256 devices in a mesh: ctx: 64 (over y, x, z_lo, core), head: 4 (over z_hi).
Axes of the slice: x: 4, y: 4, z: 8 (z_hi: 4, z_lo: 2; z = z_hi * 2 + z_lo), core: 2. Of those that a mesh axis runs over, the one named last changes fastest.
Arguments:
- query_states: bfloat16 [32768, 2048], P('ctx', 'head'), may hold values from -8 to 8
- key_states: bfloat16 [32768, 2048], P('ctx', 'head'), may hold values from -8 to 8
- value_states: bfloat16 [32768, 2048], P('ctx', 'head'), may hold values from -6 to 6
- offsets: int32 [6, 16], replicated, may hold values from 0 to 31, as said below
- out_weight: bfloat16 [2048, 2048], P('head'), may hold values from -0.125 to 0.125
Outputs:
- layer_out: bfloat16 [32768, 2048], P('ctx', 'head')
The draws below stay inside these ranges and needn't reach their ends.
Inputs may be any that keep to these rules, and one draw needn't show every extreme that they name: offsets[l, h] lies in 0 to 2**l - 1; at level 5 some head takes 2**5 - 1.
All inputs are finite; a program needn't handle non-finite values.
Results may differ from the reference program's by a relative error of at most 0.0053.
Values may be sent and summed in bfloat16 or wider, within the bound.
No kernel may reach another device: no remote copies, remote signals or barrier semaphores. Data moves between devices by JAX's collectives and lax.ppermute only.
A program may use at most 128 MiB of HBM per device.

```python
import math
import jax
import jax.numpy as jnp
from jax import lax

D = 2048
H = 16
HD = 128
TOK_DEV = 512
LEVELS = 6
TOKENS = 32768


def drawn_rows(key):
    states = jax.random.normal(key, (TOKENS, H * HD), jnp.float32)
    return jnp.clip(states, -6.0, 6.0).astype(jnp.bfloat16)


def draw_query_states(key, part):
    key = jax.random.fold_in(key, 21)
    return drawn_rows(key)


def draw_key_states(key, part):
    key = jax.random.fold_in(key, 22)
    return drawn_rows(key)


def draw_offsets(key, part):
    key = jax.random.fold_in(key, 23)
    values_key, head_key = jax.random.split(key)
    raw_values = jax.random.randint(values_key, (LEVELS, H), 0, 2 ** 20, dtype=jnp.int32)
    level_spans = jnp.left_shift(jnp.ones((LEVELS,), jnp.int32), jnp.arange(LEVELS, dtype=jnp.int32))
    drawn_values = raw_values % level_spans[:, None]
    forced_head = jax.random.randint(head_key, (), 0, H, dtype=jnp.int32)
    last_entry = (jnp.arange(LEVELS, dtype=jnp.int32)[:, None] == LEVELS - 1) & (jnp.arange(H, dtype=jnp.int32)[None, :] == forced_head)
    return jnp.where(last_entry, 2 ** (LEVELS - 1) - 1, drawn_values).astype(jnp.int32)


def level_of(own_key, extent, cuts, least, high):
    gain, own = 1.0, jax.random.fold_in(own_key, 6)
    for dim, shards_of in cuts:
        draws = jnp.exp(jax.random.uniform(jax.random.fold_in(own, dim), (shards_of,), jnp.float32, least / len(cuts), high / len(cuts)))
        gain = gain * jnp.repeat(draws, extent[dim] // shards_of).reshape([-1 if axis == dim else 1 for axis in range(len(extent))])
    return gain


def centred(rng, dims, scale, reach, pieces=(), kind=jnp.bfloat16):
    result = scale * jax.random.normal(rng, dims, jnp.float32)
    if pieces:
        result = result * level_of(rng, dims, pieces, -0.22, 0.18)
    return jnp.clip(result, -reach, reach).astype(kind)


def setup_inputs(seed: int = 0) -> dict:
    keys = jax.random.split(jax.random.key(seed), 6)
    query_states = draw_query_states(jax.random.fold_in(keys[5], 71), 0)
    key_states = draw_key_states(jax.random.fold_in(keys[5], 71), 0)
    value_states = centred(keys[2], (TOKENS, H * HD), 1.0, 6.0, ((0, 64), (1, 4)))
    offsets = draw_offsets(jax.random.fold_in(keys[5], 71), 0)
    out_weight = centred(keys[4], (H * HD, D), (H * HD) ** -0.5, 0.125, ((0, 4),))
    return {"query_states": query_states, "key_states": key_states, "value_states": value_states, "offsets": offsets, "out_weight": out_weight}


def pick_rows(series, offset, dilation):
    grouped = series.reshape(TOKENS // dilation, dilation, HD)
    chosen = lax.dynamic_index_in_dim(grouped, offset, 1, False)
    return chosen.reshape(TOKENS // (dilation * TOK_DEV), TOK_DEV, HD)

def place_rows(flat_rows, offset, dilation, filler):
    remaining_tail = flat_rows.shape[1:]
    grouped = jnp.full((TOKENS // dilation, dilation) + remaining_tail, filler, jnp.float32)
    update = flat_rows.reshape((TOKENS // dilation, 1) + remaining_tail)
    placed = lax.dynamic_update_index_in_dim(grouped, update, offset, 1)
    return placed.reshape((TOKENS,) + remaining_tail)

def segment_attention(query_seg, key_seg, value_seg):
    scale_factor = 1.0 / math.sqrt(HD)
    scores = jnp.einsum('snd,smd->snm', query_seg.astype(jnp.float32), key_seg.astype(jnp.float32)) * scale_factor
    causal = jnp.tril(jnp.ones((TOK_DEV, TOK_DEV), jnp.bool_))
    scores = jnp.where(causal[None], scores, -jnp.inf)
    peak = lax.optimization_barrier(jnp.max(scores, axis=-1, keepdims=True))
    expo = jnp.exp(scores - peak)
    total = lax.optimization_barrier(jnp.sum(expo, axis=-1, keepdims=True))
    weight_matrix = lax.optimization_barrier(expo.astype(jnp.bfloat16)).astype(jnp.float32)
    level_mixed = jnp.einsum('snm,smd->snd', weight_matrix, value_seg.astype(jnp.float32)) / total
    return (level_mixed, peak[..., 0] + jnp.log(total[..., 0]))

def head_attention(packed):
    query_head, key_head, value_head, head_offsets = packed
    outputs = []
    lse_list = []
    for level_index in range(LEVELS):
        dilation = 2 ** level_index
        offset = head_offsets[level_index]
        level_mixed, level_lse = segment_attention(pick_rows(query_head, offset, dilation), pick_rows(key_head, offset, dilation), pick_rows(value_head, offset, dilation))
        outputs.append(place_rows(level_mixed.reshape(TOKENS // dilation, HD), offset, dilation, 0.0))
        lse_list.append(place_rows(level_lse.reshape(TOKENS // dilation), offset, dilation, -jnp.inf))
    stacked_lse = jnp.stack(lse_list)
    top_lse = lax.optimization_barrier(jnp.max(stacked_lse, axis=0))
    shares = jnp.exp(stacked_lse - top_lse[None])
    numer = lax.optimization_barrier(jnp.sum(shares[..., None] * jnp.stack(outputs), axis=0))
    denom = lax.optimization_barrier(jnp.sum(shares, axis=0))
    return (numer / denom[:, None]).astype(jnp.bfloat16)

def split_heads(states):
    return jnp.moveaxis(states.reshape(TOKENS, H, HD), 1, 0)

def reference(query_states, key_states, value_states, offsets, out_weight):
    attended = lax.map(head_attention, (split_heads(query_states), split_heads(key_states), split_heads(value_states), offsets.T))
    attended = jnp.moveaxis(attended, 0, 1).reshape(TOKENS, H * HD)
    return jnp.dot(attended, out_weight, preferred_element_type=jnp.float32).astype(jnp.bfloat16)
```

```python
import functools
import math

import jax
import jax.numpy as jnp
from jax import lax
from jax.experimental import pallas as pl
from jax.experimental.pallas import tpu as pltpu
from jax.sharding import PartitionSpec as P

HD = 128
F32 = jnp.float32
BF16 = jnp.bfloat16
TOK = 512
CHIP = 2 * TOK
GAIN = math.log2(math.e) / math.sqrt(HD)
CORE, Z, X1, X2, Y1 = 1, 2, 4, 8, 16
BLOCKS = {
    2: (0, 1),
    3: (0, 1, 2, 3),
    4: (0, 2, 4, 6, 1, 3, 5, 7),
    5: (0, 2, 4, 6, 1, 3, 5, 7, 8, 10, 12, 14, 9, 11, 13, 15),
}


def swap(block, bits, up_only=False):
    route = [(i, i ^ bits) for i in range(64) if not up_only or i < i ^ bits]
    return lax.ppermute(block, "ctx", route)


def ring(block, step):
    return lax.ppermute(block, "head", [(i, (i + step) % 4) for i in range(4)])


def params():
    return pltpu.CompilerParams(vmem_limit_bytes=24 * 1024 * 1024)


def used(off, level, j, first=0, count=None):
    r = 1 << level
    n = CHIP // r if count is None else count
    return pl.ds(off + first * r, n, stride=r)


def fill(buf, base, pos, mine, theirs):
    core = pos[0]
    here = pl.multiple_of(core * TOK, TOK)
    there = pl.multiple_of(TOK - core * TOK, TOK)
    for j in range(2):
        cols = pl.ds(pl.multiple_of(core * 256 + j * HD, HD), HD)
        buf[base + j, pl.ds(here, TOK), :] = mine[:, cols].astype(F32)
        buf[base + j, pl.ds(there, TOK), :] = theirs[:, j * HD : (j + 1) * HD].astype(F32)


def pick_kernel(pos, offs, k, v, rk, rv, g45, g3, g2, buf):
    fill(buf, 0, pos, k, rk)
    fill(buf, 2, pos, v, rv)
    for level, dst, row in ((5, g45, 0), (4, g45, 64), (3, g3, 0), (2, g2, 0)):
        n = CHIP >> level
        for j in range(2):
            rows = used(offs[level, pos[1] + j], level, j)
            dst[row + j * n : row + (j + 1) * n, :HD] = buf[j, rows, :].astype(BF16)
            dst[row + j * n : row + (j + 1) * n, HD:] = buf[2 + j, rows, :].astype(BF16)


def softmax_parts(scores, values):
    peak = jnp.max(scores, axis=-1, keepdims=True)
    expo = jnp.exp2((scores - peak) * GAIN)
    total = jnp.sum(expo, axis=-1, keepdims=True)
    mixed = jnp.dot(expo.astype(BF16), values, preferred_element_type=F32)
    return peak, total, mixed


def raw_scores(q, k):
    return lax.dot_general(q, k, (((1,), (1,)), ((), ())), preferred_element_type=F32)


def causal(q, k, v, first):
    n = q.shape[0]
    m = first + n
    s = raw_scores(q, k[:m])
    row = lax.broadcasted_iota(jnp.int32, (n, m), 0) + first
    col = lax.broadcasted_iota(jnp.int32, (n, m), 1)
    s = jnp.where(col <= row, s, -jnp.inf)
    return softmax_parts(s, v[:m])


def pack(peak, total):
    lane = lax.broadcasted_iota(jnp.int32, (peak.shape[0], HD), 1)
    return jnp.where(lane < HD // 2, peak, total)


def merge(acc, stat, j, rows, peak, total, mixed):
    old = stat[j, rows, :]
    old_peak, old_total = old[:, :1], old[:, HD // 2 : HD // 2 + 1]
    top = jnp.maximum(old_peak, peak)
    a = jnp.exp2((old_peak - top) * GAIN)
    b = jnp.exp2((peak - top) * GAIN)
    acc[j, rows, :] = acc[j, rows, :] * a + mixed * b
    stat[j, rows, :] = pack(top, old_total * a + total * b)


def near_kernel(pos, offs, q, k, v, rq, rk, rv, acc, stat, bq, buf):
    fill(buf, 0, pos, q, rq)
    fill(buf, 2, pos, k, rk)
    fill(buf, 4, pos, v, rv)
    row = 0
    for level in (5, 4, 3, 2):
        n = CHIP >> level
        for j in range(2):
            rows = used(offs[level, pos[1] + j], level, j)
            bq[row : row + n, :] = buf[j, rows, :].astype(BF16)
            row += n
    for j in range(2):
        for tile in range(2):
            span = slice(tile * TOK, (tile + 1) * TOK)
            qs, ks, vs = (buf[2 * i + j, span, :].astype(BF16) for i in range(3))
            for half in range(2):
                peak, total, mixed = causal(qs[half * 256 : half * 256 + 256], ks, vs, half * 256)
                at = slice(tile * TOK + half * 256, tile * TOK + half * 256 + 256)
                acc[j, at, :] = mixed
                stat[j, at, :] = pack(peak, total)
    for j in range(2):
        off = offs[1, pos[1] + j]
        qs, ks, vs = (buf[2 * i + j, used(off, 1, j), :].astype(BF16) for i in range(3))
        for half in range(2):
            part = causal(qs[half * 256 : half * 256 + 256], ks, vs, half * 256)
            merge(acc, stat, j, used(off, 1, j, half * 256, 256), *part)


def far_kernel(pos, offs, bias, acc0, stat0, bq, o45, o3, o2, a0, a1, a2, b, c, d, e, f, g, mine, other, acc, stat):
    acc[...] = acc0[...]
    stat[...] = stat0[...]
    quad = (o45, a0, a1, a2)
    for level in (2, 3, 4, 5):
        n = CHIP >> level
        qrow = {5: 0, 4: 64, 3: 192, 2: 448}[level]
        for j in range(2):
            at = slice(j * n, (j + 1) * n)
            if level == 2:
                parts = [o2[at], c[at]]
            elif level == 3:
                parts = [o3[at], b[at], d[at], d[256 + j * n : 256 + (j + 1) * n]]
            else:
                s = 64 if level == 4 else 0
                at = slice(s + j * n, s + (j + 1) * n)
                parts = [x[at] for x in quad]
                parts += [e[192 * i + s + j * n : 192 * i + s + (j + 1) * n] for i in range(4)]
                if level == 5:
                    for y in (f, g):
                        parts += [y[64 * i + j * n : 64 * i + (j + 1) * n] for i in range(4)]
            keys = jnp.concatenate([x[:, :HD] for x in parts], axis=0)
            values = jnp.concatenate([x[:, HD:] for x in parts], axis=0)
            s = raw_scores(bq[qrow + j * n : qrow + (j + 1) * n, :], keys)
            row = lax.broadcasted_iota(jnp.int32, s.shape, 0)
            col = lax.broadcasted_iota(jnp.int32, s.shape, 1)
            s = s + bias[level : level + 1, :]
            s = jnp.where((col < n) & (col > row), -jnp.inf, s)
            part = softmax_parts(s, values)
            merge(acc, stat, j, used(offs[level, pos[1] + j], level, j), *part)
    core = pos[0]
    for start, dst in ((core * TOK, mine), (TOK - core * TOK, other)):
        rows = pl.ds(pl.multiple_of(start, TOK), TOK)
        for j in range(2):
            total = stat[j, rows, :][:, HD // 2 : HD // 2 + 1]
            dst[:, j * HD : (j + 1) * HD] = (acc[j, rows, :] / total).astype(BF16)


def project(pos, mine, back, w, first, count, dest):
    core = pos[0]
    cols = pl.ds(pl.multiple_of(dest * TOK, TOK), TOK)
    near = pl.ds(pl.multiple_of(core * 256, 256), 256)
    far = pl.ds(pl.multiple_of(256 - core * 256, 256), 256)
    rows = slice(first, first + count)
    return jnp.dot(mine[rows, :], w[near, cols], preferred_element_type=F32) + jnp.dot(
        back[rows, :], w[far, cols], preferred_element_type=F32
    )


def opposite_kernel(pos, mine, back, w, up, down):
    dest = lax.rem(pos[3] + 2, 4)
    up[...] = project(pos, mine, back, w, 0, 256, dest).astype(BF16)
    down[...] = project(pos, mine, back, w, 256, 256, dest).astype(BF16)


def rest_kernel(pos, mine, back, w, up, down, up_late, down_late, own):
    after, before = lax.rem(pos[3] + 1, 4), lax.rem(pos[3] + 3, 4)
    up[...] = project(pos, mine, back, w, 256, 256, after).astype(BF16)
    down[...] = project(pos, mine, back, w, 0, 256, before).astype(BF16)
    up_late[...] = project(pos, mine, back, w, 0, 256, after)
    down_late[...] = project(pos, mine, back, w, 256, 256, before)
    for first in (0, 256):
        own[first : first + 256, :] = project(pos, mine, back, w, first, 256, pos[3])


SMEM = pl.BlockSpec(memory_space=pltpu.SMEM)
VMEM = pl.BlockSpec(memory_space=pltpu.VMEM)


def call(kernel, scalars, arrays, outs, scratch=(), flops=0, exps=0):
    nbytes = sum(a.size * a.dtype.itemsize for a in arrays)
    return pl.pallas_call(
        kernel,
        in_specs=[SMEM] * len(scalars) + [VMEM] * len(arrays),
        out_specs=[VMEM] * len(outs),
        out_shape=[jax.ShapeDtypeStruct(s, t) for s, t in outs],
        scratch_shapes=[pltpu.VMEM(s, F32) for s in scratch],
        compiler_params=params(),
        cost_estimate=pl.CostEstimate(flops=flops, bytes_accessed=nbytes, transcendentals=exps),
    )(*scalars, *arrays)


def local(q, k, v, offsets, w):
    ctx = lax.axis_index("ctx")
    head = lax.axis_index("head")
    core = ctx % 2
    chip = ctx // 2
    pos = jnp.stack([core, head * 4 + core * 2, chip, head]).astype(jnp.int32)

    def theirs(x):
        return lax.dynamic_slice_in_dim(x, 256 - core * 256, 256, 1)

    rk, rv, rq = (swap(theirs(x), CORE) for x in (k, v, q))
    g45, g3, g2 = call(
        pick_kernel,
        (pos, offsets),
        (k, v, rk, rv),
        [((192, 256), BF16), ((256, 256), BF16), ((512, 256), BF16)],
        [(4, CHIP, HD)],
    )
    a = [swap(g45, bits) for bits in (X1, X2, X1 | X2)]
    b = swap(g3, Z)
    c = swap(g2, Z, True)
    acc, stat, bq = call(
        near_kernel,
        (pos, offsets),
        (q, k, v, rq, rk, rv),
        [((2, CHIP, HD), F32), ((2, CHIP, HD), F32), ((960, HD), BF16)],
        [(6, CHIP, HD)],
        flops=6 * 4 * TOK * TOK * HD,
        exps=6 * TOK * TOK,
    )
    d = swap(jnp.concatenate([g3, b]), X1, True)
    e = swap(jnp.concatenate([g45] + a), Z)
    g5 = jnp.concatenate([g45[:64]] + [x[:64] for x in a])
    f = swap(g5, Y1, True)
    g = swap(g5, Y1 | Z, True)

    rows = [jnp.zeros((2, TOK), F32)]
    for level in (2, 3, 4, 5):
        span = chip % (1 << (level - 1))
        code = jnp.array(BLOCKS[level], jnp.int32)
        fine = (code == 0) | ((span ^ code) < span)
        rows.append(jnp.repeat(jnp.where(fine, 0.0, -jnp.inf).astype(F32), CHIP >> level)[None])
    bias = jnp.concatenate(rows)

    mine, other = call(
        far_kernel,
        (pos, offsets),
        (bias, acc, stat, bq, g45, g3, g2, *a, b, c, d, e, f, g),
        [((TOK, 256), BF16), ((TOK, 256), BF16)],
        [(2, CHIP, HD), (2, CHIP, HD)],
        flops=2 * 4 * TOK * TOK * HD,
        exps=2 * TOK * TOK,
    )
    back = swap(other, CORE)

    half = (256, TOK)
    up1, down1 = call(
        opposite_kernel, (pos,), (mine, back, w), [(half, BF16)] * 2, flops=2 * TOK * TOK * TOK
    )
    up1, down1 = ring(up1, 1), ring(down1, 3)
    up2, down2, up_late, down_late, own = call(
        rest_kernel,
        (pos,),
        (mine, back, w),
        [(half, BF16)] * 2 + [(half, F32)] * 2 + [((TOK, TOK), F32)],
        flops=6 * TOK * TOK * TOK,
    )
    up2, down2 = ring(up2, 1), ring(down2, 3)
    up3 = ring((up_late + up1.astype(F32)).astype(BF16), 1)
    down3 = ring((down_late + down1.astype(F32)).astype(BF16), 3)
    top = own[:256] + up3.astype(F32) + down2.astype(F32)
    bottom = own[256:] + up2.astype(F32) + down3.astype(F32)
    return jnp.concatenate([top, bottom]).astype(BF16)


def solution(mesh):
    placed = (P("ctx", "head"), P("ctx", "head"), P("ctx", "head"), P(), P("head", None))
    return jax.shard_map(
        local, mesh=mesh, in_specs=placed, out_specs=P("ctx", "head"), check_vma=False
    )
```

```python
import math

import jax
import jax.numpy as jnp
from jax import lax
from jax.experimental import pallas as pl
from jax.experimental.pallas import tpu as pltpu
from jax.sharding import PartitionSpec as P

HD = 128
F32 = jnp.float32
BF16 = jnp.bfloat16
TOK = 512
CHIP = 2 * TOK
GAIN = math.log2(math.e) / math.sqrt(HD)
CORE, Z, X1, X2, Y1 = 1, 2, 4, 8, 16


def swap(block, bits):
    return lax.ppermute(block, "ctx", [(i, i ^ bits) for i in range(64)])


def cross(block, bits):
    return lax.ppermute(block, "head", [(i, i ^ bits) for i in range(4)])


def used(off, level, first=0, count=None):
    r = 1 << level
    n = CHIP // r if count is None else count
    return pl.ds(off + first * r, n, stride=r)


def halves(pos):
    here = pl.multiple_of(pos[0] * TOK, TOK)
    there = pl.multiple_of(TOK - pos[0] * TOK, TOK)
    return pl.ds(here, TOK), pl.ds(there, TOK)


def split_kernel(pos, q, k, v, okv, oq, mkv, mq, sems):
    mine = pl.ds(pl.multiple_of(pos[0] * 256, 256), 256)
    theirs = pl.ds(pl.multiple_of(256 - pos[0] * 256, 256), 256)
    moves = (
        (k, theirs, okv.at[0]),
        (v, theirs, okv.at[1]),
        (q, theirs, oq),
        (k, mine, mkv.at[0]),
        (v, mine, mkv.at[1]),
        (q, mine, mq),
    )
    copies = [
        pltpu.make_async_copy(src.at[:, cols], dst, sems.at[i])
        for i, (src, cols, dst) in enumerate(moves)
    ]
    for copy in copies:
        copy.start()
    for copy in copies:
        copy.wait()


def fill(buf, base, pos, mine, theirs):
    here, there = halves(pos)
    for j in range(2):
        cols = slice(j * HD, (j + 1) * HD)
        buf[base + j, here, :] = mine[:, cols].astype(F32)
        buf[base + j, there, :] = theirs[:, cols].astype(F32)


def pick_kernel(pos, offs, mkv, rkv, after, g45, g345, g32, buf):
    del after
    for i in range(2):
        fill(buf, 2 * i, pos, mkv.at[i], rkv.at[i])
    places = {5: ((g45, 0), (g345, 0)), 4: ((g45, 64), (g345, 64)), 3: ((g345, 192), (g32, 0)), 2: ((g32, 256),)}
    for level, where in places.items():
        n = CHIP >> level
        for j in range(2):
            rows = used(offs[level, pos[1] + j], level)
            for i in range(2):
                part = buf[2 * i + j, rows, :].astype(BF16)
                for dst, row in where:
                    dst[row + j * n : row + (j + 1) * n, i * HD : (i + 1) * HD] = part


def softmax_parts(scores, values):
    peak = jnp.max(scores, axis=-1, keepdims=True)
    expo = jnp.exp2((scores - peak) * GAIN)
    total = jnp.sum(expo, axis=-1, keepdims=True)
    mixed = jnp.dot(expo.astype(BF16), values, preferred_element_type=F32)
    return peak, total, mixed


def raw_scores(q, k):
    return lax.dot_general(q, k, (((1,), (1,)), ((), ())), preferred_element_type=F32)


def causal(q, k, v, half):
    n = q.shape[0]
    row = lax.broadcasted_iota(jnp.int32, (n, n), 0)
    col = lax.broadcasted_iota(jnp.int32, (n, n), 1)
    s = jnp.where(col <= row, raw_scores(q, k[half * n : (half + 1) * n]), -jnp.inf)
    if half:
        s = jnp.concatenate([raw_scores(q, k[:n]), s], axis=1)
    return softmax_parts(s, v[: (half + 1) * n])


def pack(peak, total):
    lane = lax.broadcasted_iota(jnp.int32, (peak.shape[0], HD), 1)
    return jnp.where(lane < HD // 2, peak, total)


def merge(acc, stat, j, rows, peak, total, mixed):
    old = stat[j, rows, :]
    old_peak, old_total = old[:, :1], old[:, HD // 2 : HD // 2 + 1]
    top = jnp.maximum(old_peak, peak)
    a = jnp.exp2((old_peak - top) * GAIN)
    b = jnp.exp2((peak - top) * GAIN)
    acc[j, rows, :] = acc[j, rows, :] * a + mixed * b
    stat[j, rows, :] = pack(top, old_total * a + total * b)


def tile_kernel(q, kv, after, acc, stat):
    del after
    for j in range(2):
        cols = slice(j * HD, (j + 1) * HD)
        for half in range(2):
            at = slice(half * 256, half * 256 + 256)
            peak, total, mixed = causal(q[at, cols], kv[0, :, cols], kv[1, :, cols], half)
            acc[j, at, :] = mixed
            stat[j, at, :] = pack(peak, total)


def regroup_kernel(g45, a0, a1, a2, zb, after, e, g5, d):
    del after
    for i, part in enumerate((g45, a0, a1, a2)):
        e[192 * i : 192 * (i + 1), :] = part[:192, :]
        g5[64 * i : 64 * (i + 1), :] = part[:64, :]
    d[...] = zb[:256, :]


def far_scores(pos, q, keys, level):
    n = q.shape[0]
    span = lax.rem(pos[2], 1 << (level - 1))
    block = lax.broadcasted_iota(jnp.int32, (1, TOK), 1) // n
    if level <= 3:
        code = block
    else:
        code = ((block & 3) << 1) | ((block >> 2) & 1) | (block & 8)
    bias = jnp.where((block == 0) | ((span ^ code) < span), 0.0, -jnp.inf)
    s = raw_scores(q, keys) + bias
    row = lax.broadcasted_iota(jnp.int32, s.shape, 0)
    col = lax.broadcasted_iota(jnp.int32, s.shape, 1)
    return jnp.where((col < n) & (col > row), -jnp.inf, s)


def far_level(pos, offs, acc, stat, level, j, q, parts):
    keys = jnp.concatenate([x[:, :HD] for x in parts], axis=0)
    values = jnp.concatenate([x[:, HD:] for x in parts], axis=0)
    part = softmax_parts(far_scores(pos, q, keys, level), values)
    merge(acc, stat, j, used(offs[level, pos[1] + j], level), *part)


def near_kernel(pos, offs, mq, mkv, rq, rkv, acc_m, stat_m, acc_r, stat_r, g32, zb, after, acc, stat, bq, buf):
    del after
    fill(buf, 0, pos, mq, rq)
    for i in range(2):
        fill(buf, 2 + 2 * i, pos, mkv.at[i], rkv.at[i])
    here, there = halves(pos)
    for j in range(2):
        acc[j, here, :] = acc_m[j]
        acc[j, there, :] = acc_r[j]
        stat[j, here, :] = stat_m[j]
        stat[j, there, :] = stat_r[j]
    row = 0
    for level in (5, 4, 3):
        n = CHIP >> level
        for j in range(2):
            bq[row : row + n, :] = buf[j, used(offs[level, pos[1] + j], level), :].astype(BF16)
            row += n
    for j in range(2):
        off = offs[1, pos[1] + j]
        qs, ks, vs = (buf[2 * i + j, used(off, 1), :].astype(BF16) for i in range(3))
        for half in range(2):
            part = causal(qs[half * 256 : half * 256 + 256], ks, vs, half)
            merge(acc, stat, j, used(off, 1, half * 256, 256), *part)
    for j in range(2):
        at = slice(256 + j * 256, 512 + j * 256)
        q = buf[j, used(offs[2, pos[1] + j], 2), :].astype(BF16)
        far_level(pos, offs, acc, stat, 2, j, q, [g32[at], zb[at]])


def far_kernel(pos, offs, acc0, stat0, bq, g45, g32, a0, a1, a2, zb, d, e, f, g, mine, other, acc, stat):
    acc[...] = acc0[...]
    stat[...] = stat0[...]
    quad = (g45, a0, a1, a2)
    for level in (3, 4, 5):
        n = CHIP >> level
        qrow = {5: 0, 4: 64, 3: 192}[level]
        for j in range(2):
            at = slice(j * n, (j + 1) * n)
            if level == 3:
                parts = [g32[at], zb[at], a0[192 + j * n : 192 + (j + 1) * n], d[at]]
            else:
                s = 64 if level == 4 else 0
                at = slice(s + j * n, s + (j + 1) * n)
                parts = [x[at] for x in quad]
                parts += [e[192 * i + s + j * n : 192 * i + s + (j + 1) * n] for i in range(4)]
                if level == 5:
                    for y in (f, g):
                        parts += [y[64 * i + j * n : 64 * i + (j + 1) * n] for i in range(4)]
            q = bq[qrow + j * n : qrow + (j + 1) * n, :]
            far_level(pos, offs, acc, stat, level, j, q, parts)
    here, there = halves(pos)
    for rows, dst in ((there, other), (here, mine)):
        for j in range(2):
            total = stat[j, rows, :][:, HD // 2 : HD // 2 + 1]
            dst[:, j * HD : (j + 1) * HD] = (acc[j, rows, :] / total).astype(BF16)


def project(pos, mine, back, w, first, dest):
    cols = pl.ds(pl.multiple_of(dest * TOK, TOK), TOK)
    near = pl.ds(pl.multiple_of(pos[0] * 256, 256), 256)
    far = pl.ds(pl.multiple_of(256 - pos[0] * 256, 256), 256)
    rows = slice(first, first + 256)
    return jnp.dot(mine[rows, :], w[near, cols], preferred_element_type=F32) + jnp.dot(
        back[rows, :], w[far, cols], preferred_element_type=F32
    )


def opposite_kernel(pos, mine, back, w, up, down):
    up[...] = project(pos, mine, back, w, 0, pos[3] ^ 2).astype(BF16)
    down[...] = project(pos, mine, back, w, 256, pos[3] ^ 2).astype(BF16)


def rest_kernel(pos, mine, back, w, after, up, down, up_late, down_late, own):
    del after
    up[...] = project(pos, mine, back, w, 0, pos[3] ^ 1).astype(BF16)
    down[...] = project(pos, mine, back, w, 256, pos[3] ^ 3).astype(BF16)
    up_late[...] = project(pos, mine, back, w, 0, pos[3] ^ 3)
    down_late[...] = project(pos, mine, back, w, 256, pos[3] ^ 1)
    for first in (0, 256):
        own[first : first + 256, :] = project(pos, mine, back, w, first, pos[3])


def relay_kernel(late, came, out):
    out[...] = (late[...] + came[...].astype(F32)).astype(BF16)


def final_kernel(own, up2, up3, down2, down3, out):
    out[:256, :] = (own[:256, :] + up2[...].astype(F32) + up3[...].astype(F32)).astype(BF16)
    out[256:, :] = (own[256:, :] + down2[...].astype(F32) + down3[...].astype(F32)).astype(BF16)


SMEM = pl.BlockSpec(memory_space=pltpu.SMEM)
VMEM = pl.BlockSpec(memory_space=pltpu.VMEM)
ANY = pl.BlockSpec(memory_space=pl.ANY)


def call(kernel, scalars, arrays, outs, scratch=(), flops=0, exps=0, unread=(), anywhere=False):
    nbytes = sum(a.size * a.dtype.itemsize for a in arrays)
    shapes = [s if not isinstance(s, tuple) else pltpu.VMEM(s, F32) for s in scratch]
    return pl.pallas_call(
        kernel,
        in_specs=[SMEM] * len(scalars)
        + [ANY if anywhere else VMEM] * len(arrays)
        + [ANY] * len(unread),
        out_specs=[VMEM] * len(outs),
        out_shape=[jax.ShapeDtypeStruct(s, t) for s, t in outs],
        scratch_shapes=shapes,
        compiler_params=pltpu.CompilerParams(vmem_limit_bytes=24 * 1024 * 1024),
        cost_estimate=pl.CostEstimate(flops=flops, bytes_accessed=nbytes, transcendentals=exps),
    )(*scalars, *arrays, *unread)


def local(q, k, v, offsets, w):
    ctx = lax.axis_index("ctx")
    head = lax.axis_index("head")
    core = ctx % 2
    pos = jnp.stack([core, head * 4 + core * 2, ctx // 2, head]).astype(jnp.int32)
    unit = 4 * TOK * TOK * HD
    part = (TOK, 256)
    state = (2, TOK, HD)

    okv, oq, mkv, mq = call(
        split_kernel,
        (pos,),
        (q, k, v),
        [((2,) + part, BF16), (part, BF16)] * 2,
        [pltpu.SemaphoreType.DMA((6,))],
        anywhere=True,
    )
    rkv, rq = swap(okv, CORE), swap(oq, CORE)
    acc_m, stat_m = call(tile_kernel, (), (mq, mkv), [(state, F32)] * 2, flops=2 * unit, unread=(oq,))
    g45, g345, g32 = call(
        pick_kernel,
        (pos, offsets),
        (mkv, rkv),
        [((192, 256), BF16), ((448, 256), BF16), ((768, 256), BF16)],
        [(4, CHIP, HD)],
        unread=(acc_m,),
    )
    zb = swap(g32, Z)
    a0, a1, a2 = swap(g345, X1), swap(g45, X2), swap(g45, X1 | X2)
    acc_r, stat_r = call(tile_kernel, (), (rq, rkv), [(state, F32)] * 2, flops=2 * unit, unread=(g45,))
    e, g5, d = call(
        regroup_kernel,
        (),
        (g45, a0, a1, a2, zb),
        [((768, 256), BF16), ((256, 256), BF16), ((256, 256), BF16)],
        unread=(acc_r,),
    )
    far_e, far_f, far_g, far_d = swap(e, Z), swap(g5, Y1), swap(g5, Y1 | Z), swap(d, X1)
    acc, stat, bq = call(
        near_kernel,
        (pos, offsets),
        (mq, mkv, rq, rkv, acc_m, stat_m, acc_r, stat_r, g32, zb),
        [((2, CHIP, HD), F32), ((2, CHIP, HD), F32), ((448, HD), BF16)],
        [(6, CHIP, HD)],
        flops=3 * unit,
        unread=(g5,),
    )
    mine, other = call(
        far_kernel,
        (pos, offsets),
        (acc, stat, bq, g45, g32, a0, a1, a2, zb, far_d, far_e, far_f, far_g),
        [(part, BF16)] * 2,
        [(2, CHIP, HD), (2, CHIP, HD)],
        flops=unit,
    )
    back = swap(other, CORE)

    half = (256, TOK)
    up1, down1 = call(opposite_kernel, (pos,), (mine, back, w), [(half, BF16)] * 2, flops=2 * TOK**3)
    came_up, came_down = cross(up1, 1), cross(down1, 3)
    up2, down2, up_late, down_late, own = call(
        rest_kernel,
        (pos,),
        (mine, back, w),
        [(half, BF16)] * 2 + [(half, F32)] * 2 + [((TOK, TOK), F32)],
        flops=6 * TOK**3,
        unread=(up1,),
    )
    up2, down2 = cross(up2, 1), cross(down2, 3)
    up3 = cross(call(relay_kernel, (), (up_late, came_up), [(half, BF16)])[0], 3)
    down3 = cross(call(relay_kernel, (), (down_late, came_down), [(half, BF16)])[0], 1)
    return call(final_kernel, (), (own, up2, up3, down2, down3), [((TOK, TOK), BF16)])[0]


def solution(mesh):
    placed = (P("ctx", "head"), P("ctx", "head"), P("ctx", "head"), P(), P("head", None))
    return jax.shard_map(
        local, mesh=mesh, in_specs=placed, out_specs=P("ctx", "head"), check_vma=False
    )
```

```python
import math

import jax
import jax.numpy as jnp
from jax import lax
from jax.experimental import pallas as pl
from jax.experimental.pallas import tpu as pltpu
from jax.sharding import PartitionSpec as P

HD = 128
F32 = jnp.float32
BF16 = jnp.bfloat16
TOK = 512
CHIP = 2 * TOK
MIB = 1024 * 1024
GAIN = math.log2(math.e) / math.sqrt(HD)
CORE, Z, X1, X2, Y1 = 1, 2, 4, 8, 16


def swap(block, bits):
    return lax.ppermute(block, "ctx", [(i, i ^ bits) for i in range(64)])


def cross(block, bits):
    return lax.ppermute(block, "head", [(i, i ^ bits) for i in range(4)])


def used(off, level, first=0, count=None):
    r = 1 << level
    n = CHIP // r if count is None else count
    return pl.ds(off + first * r, n, stride=r)


def halves(pos):
    here = pl.multiple_of(pos[0] * TOK, TOK)
    there = pl.multiple_of(TOK - pos[0] * TOK, TOK)
    return pl.ds(here, TOK), pl.ds(there, TOK)


def run_copies(moves, sems):
    copies = [pltpu.make_async_copy(src, dst, sems.at[i]) for i, (src, dst) in enumerate(moves)]
    for copy in copies:
        copy.start()
    for copy in copies:
        copy.wait()


def theirs_kernel(k, v, okv, sems):
    core = lax.rem(lax.axis_index("ctx"), 2)
    theirs = pl.ds(pl.multiple_of(256 - core * 256, 256), 256)
    run_copies([(k.at[:, theirs], okv.at[0]), (v.at[:, theirs], okv.at[1])], sems)


def mine_columns_kernel(q, k, v, after, oq, mkv, mq, sems):
    del after
    core = lax.rem(lax.axis_index("ctx"), 2)
    theirs = pl.ds(pl.multiple_of(256 - core * 256, 256), 256)
    mine = pl.ds(pl.multiple_of(core * 256, 256), 256)
    moves = [(q.at[:, theirs], oq), (q.at[:, mine], mq)]
    moves += [(k.at[:, mine], mkv.at[0]), (v.at[:, mine], mkv.at[1])]
    run_copies(moves, sems)


def fill(buf, base, pos, mine, theirs):
    here, there = halves(pos)
    for j in range(2):
        cols = slice(j * HD, (j + 1) * HD)
        buf[base + j, here, :] = mine[:, cols].astype(F32)
        buf[base + j, there, :] = theirs[:, cols].astype(F32)


def pick_kernel(pos, offs, mkv, rkv, after, g34, g2, g53, g5, buf):
    del after
    for i in range(2):
        fill(buf, 2 * i, pos, mkv.at[i], rkv.at[i])
    places = {3: ((g34, 0), (g53, 64)), 4: ((g34, 256),), 5: ((g53, 0), (g5, 0)), 2: ((g2, 0),)}
    for level, where in places.items():
        n = CHIP >> level
        for j in range(2):
            rows = used(offs[level, pos[1] + j], level)
            for i in range(2):
                part = buf[2 * i + j, rows, :].astype(BF16)
                for dst, row in where:
                    dst[row + j * n : row + (j + 1) * n, i * HD : (i + 1) * HD] = part


def raw_scores(q, k):
    return lax.dot_general(q, k, (((1,), (1,)), ((), ())), preferred_element_type=F32)


def softmax_parts(scores, values):
    peaks = [jnp.max(s, axis=-1, keepdims=True) for s in scores]
    expos = [jnp.exp2((s - m) * GAIN).astype(BF16) for s, m in zip(scores, peaks)]
    parts = []
    for m, e, v in zip(peaks, expos, values):
        wide = jnp.concatenate([v, jnp.ones_like(v)], axis=1)
        mixed = jnp.dot(e, wide, preferred_element_type=F32)
        parts.append((jnp.broadcast_to(m, (m.shape[0], HD)), mixed[:, HD:], mixed[:, :HD]))
    return parts


def causal_scores(q, k):
    row = lax.broadcasted_iota(jnp.int32, (256, 256), 0)
    col = lax.broadcasted_iota(jnp.int32, (256, 256), 1)
    first = jnp.where(col <= row, raw_scores(q[:256], k[:256]), -jnp.inf)
    last = jnp.where(col <= row, raw_scores(q[256:], k[256:]), -jnp.inf)
    return [first, jnp.concatenate([raw_scores(q[256:], k[:256]), last], axis=1)]


def merge(state, j, rows, part):
    acc, peak, total = state
    m, t, o = part
    old = peak[j, rows, :]
    top = jnp.maximum(old, m)
    a = jnp.exp2((old - top) * GAIN)
    b = jnp.exp2((m - top) * GAIN)
    acc[j, rows, :] = acc[j, rows, :] * a + o * b
    total[j, rows, :] = total[j, rows, :] * a + t * b
    peak[j, rows, :] = top


def tile(start, q, kv, state):
    acc, peak, total = state
    for j in range(2):
        cols = slice(j * HD, (j + 1) * HD)
        values = kv[1, :, cols]
        parts = softmax_parts(causal_scores(q[:, cols], kv[0, :, cols]), [values[:256], values])
        for half, (m, t, o) in enumerate(parts):
            rows = pl.ds(pl.multiple_of(start + half * 256, 256), 256)
            acc[j, rows, :] = o
            total[j, rows, :] = t
            peak[j, rows, :] = m


def own_tile_kernel(pos, q, kv, after, *state):
    del after
    tile(pos[0] * TOK, q, kv, state)


def other_tile_kernel(pos, acc0, peak0, total0, q, kv, after, *state):
    del acc0, peak0, total0, after
    tile(TOK - pos[0] * TOK, q, kv, state)


def gather_kernel(g5, a0, a1, a2, after, out):
    del after
    for i, part in enumerate((g5, a0, a1, a2)):
        out[64 * i : 64 * (i + 1), :] = part[:64, :]


def pair_kernel(g34, zb, p1, p2):
    for dst in (p1, p2):
        dst[:128, :] = g34[256:, :]
        dst[128:256, :] = zb[256:, :]
    p1[256:, :] = zb[:256, :]


def far_scores(pos, q, blocks, level):
    n = q.shape[0]
    span = lax.rem(pos[2], 1 << (level - 1))
    code = lax.broadcasted_iota(jnp.int32, (1, TOK), 1) // n
    if level == 5:
        code = ((code & 3) << 1) | ((code >> 2) & 1) | (code & 8)
    bias = jnp.where((code == 0) | ((span ^ code) < span), 0.0, -jnp.inf)
    s = raw_scores(q, jnp.concatenate([x[:, :HD] for x in blocks], axis=0)) + bias
    row = lax.broadcasted_iota(jnp.int32, s.shape, 0)
    col = lax.broadcasted_iota(jnp.int32, s.shape, 1)
    return jnp.where((col < n) & (col > row), -jnp.inf, s)


def far_values(blocks):
    return jnp.concatenate([x[:, HD:] for x in blocks], axis=0)


def near_kernel(pos, offs, acc0, peak0, total0, mq, mkv, rq, rkv, g2, z2, after, acc, peak, total, bq, buf):
    del acc0, peak0, total0, after
    state = (acc, peak, total)
    fill(buf, 0, pos, mq, rq)
    for i in range(2):
        fill(buf, 2 + 2 * i, pos, mkv.at[i], rkv.at[i])
    row = 0
    for level in (5, 4, 3):
        n = CHIP >> level
        for j in range(2):
            bq[row : row + n, :] = buf[j, used(offs[level, pos[1] + j], level), :].astype(BF16)
            row += n
    for j in range(2):
        off = offs[1, pos[1] + j]
        qs, ks, vs = (buf[2 * i + j, used(off, 1), :].astype(BF16) for i in range(3))
        parts = softmax_parts(causal_scores(qs, ks), [vs[:256], vs])
        for half, part in enumerate(parts):
            merge(state, j, used(off, 1, half * 256, 256), part)
    rows = [used(offs[2, pos[1] + j], 2) for j in range(2)]
    blocks = [[x[j * 256 : (j + 1) * 256] for x in (g2, z2)] for j in range(2)]
    scores = [far_scores(pos, buf[j, rows[j], :].astype(BF16), blocks[j], 2) for j in range(2)]
    parts = softmax_parts(scores, [far_values(b) for b in blocks])
    for j in range(2):
        merge(state, j, rows[j], parts[j])


def finish(acc, total, rows, dst):
    for j in range(2):
        dst[:, j * HD : (j + 1) * HD] = (acc[j, rows, :] * (1.0 / total[j, rows, :])).astype(BF16)


def far_kernel(
    pos, offs, acc0, peak0, total0, bq, g34, g5, a0, a1, a2, zb, h1, h2, h3, e, f, g, acc, peak, total, other
):
    del acc0, peak0, total0
    work = []
    for level, qrow in ((3, 192), (4, 64), (5, 0)):
        n = CHIP >> level
        for j in range(2):

            def cut(ref, row):
                return ref[row + j * n : row + (j + 1) * n]

            if level == 3:
                blocks = [cut(g34, 0), cut(zb, 0), cut(a0, 64), cut(h1, 256)]
            elif level == 4:
                blocks = [cut(g34, 256), cut(zb, 256)]
                blocks += [cut(x, row) for x in (h1, h2, h3) for row in (0, 128)]
            else:
                blocks = [cut(x, 0) for x in (g5, a0, a1, a2)]
                blocks += [cut(x, 64 * i) for x in (e, f, g) for i in range(4)]
            rows = used(offs[level, pos[1] + j], level)
            scores = far_scores(pos, cut(bq, qrow), blocks, level)
            work.append((j, rows, scores, far_values(blocks)))
    parts = softmax_parts([x[2] for x in work], [x[3] for x in work])
    for (j, rows, _, _), part in zip(work, parts):
        merge((acc, peak, total), j, rows, part)
    finish(acc, total, halves(pos)[1], other)


def dots(pos, far, rows, w, dest):
    start = 256 - pos[0] * 256 if far else pos[0] * 256
    at = pl.ds(pl.multiple_of(start, 256), 256)
    cols = pl.ds(pl.multiple_of(dest * TOK, TOK), TOK)
    return jnp.dot(rows, w[at, cols], preferred_element_type=F32)


def project(pos, mine, back, w, first, dest):
    rows = slice(first, first + 256)
    return dots(pos, False, mine[rows, :], w, dest) + dots(pos, True, back[rows, :], w, dest)


def mine_kernel(pos, acc, total, w, after, mine, part):
    del after
    finish(acc, total, halves(pos)[0], mine)
    part[...] = dots(pos, False, mine[...], w, pos[3] ^ 2)


def opposite_kernel(pos, part, back, w, up, down):
    up[...] = (part[:256, :] + dots(pos, True, back[:256, :], w, pos[3] ^ 2)).astype(BF16)
    down[...] = (part[256:, :] + dots(pos, True, back[256:, :], w, pos[3] ^ 2)).astype(BF16)


def rest_kernel(pos, mine, back, w, after, up, down, up_late, down_late, own):
    del after
    up[...] = project(pos, mine, back, w, 0, pos[3] ^ 1).astype(BF16)
    down[...] = project(pos, mine, back, w, 256, pos[3] ^ 3).astype(BF16)
    up_late[...] = project(pos, mine, back, w, 0, pos[3] ^ 3)
    down_late[...] = project(pos, mine, back, w, 256, pos[3] ^ 1)
    for first in (0, 256):
        own[first : first + 256, :] = project(pos, mine, back, w, first, pos[3])


def relay_kernel(late, came, out):
    out[...] = (late[...] + came[...].astype(F32)).astype(BF16)


def final_kernel(own, up2, up3, down2, down3, out, buf, sems):
    copies = []
    for i in range(4):
        rows = slice(i * 128, (i + 1) * 128)
        part = slice(i % 2 * 128, i % 2 * 128 + 128)
        a, b = (up2, up3) if i < 2 else (down2, down3)
        buf[rows, :] = (own[rows, :] + a[part, :].astype(F32) + b[part, :].astype(F32)).astype(BF16)
        copy = pltpu.make_async_copy(buf.at[rows, :], out.at[rows, :], sems.at[i])
        copy.start()
        copies.append(copy)
    for copy in copies:
        copy.wait()


SMEM = pl.BlockSpec(memory_space=pltpu.SMEM)
VMEM = pl.BlockSpec(memory_space=pltpu.VMEM)
ANY = pl.BlockSpec(memory_space=pl.ANY)


def call(
    kernel, scalars, arrays, outs, scratch=(), flops=0, unread=(), inside=VMEM, outside=VMEM, inplace=0, grant=24
):
    nbytes = sum(a.size * a.dtype.itemsize for a in arrays)
    return pl.pallas_call(
        kernel,
        in_specs=[SMEM] * len(scalars) + [inside] * len(arrays) + [ANY] * len(unread),
        out_specs=[outside] * len(outs),
        out_shape=[jax.ShapeDtypeStruct(s, t) for s, t in outs],
        scratch_shapes=list(scratch),
        input_output_aliases={len(scalars) + i: i for i in range(inplace)},
        compiler_params=pltpu.CompilerParams(vmem_limit_bytes=grant * MIB),
        cost_estimate=pl.CostEstimate(flops=flops, bytes_accessed=nbytes, transcendentals=0),
    )(*scalars, *arrays, *unread)


def local(q, k, v, offsets, w):
    ctx = lax.axis_index("ctx")
    head = lax.axis_index("head")
    core = ctx % 2
    pos = jnp.stack([core, head * 4 + core * 2, ctx // 2, head]).astype(jnp.int32)
    unit = 4 * TOK * TOK * HD
    part = (TOK, 256)

    def rows(n):
        return ((n, 256), BF16)

    q, k, v = (pltpu.with_memory_space_constraint(x, pltpu.HBM) for x in (q, k, v))
    sems = pltpu.SemaphoreType.DMA
    okv = call(theirs_kernel, (), (k, v), [((2,) + part, BF16)], [sems((2,))], inside=ANY)[0]
    rkv = swap(okv, CORE)
    oq, mkv, mq = call(
        mine_columns_kernel,
        (),
        (q, k, v),
        [(part, BF16), ((2,) + part, BF16), (part, BF16)],
        [sems((4,))],
        inside=ANY,
        unread=(okv,),
    )
    rq = swap(oq, CORE)
    states = [((2, CHIP, HD), F32)] * 3
    state = call(own_tile_kernel, (pos,), (mq, mkv), states, flops=2 * unit, unread=(oq,))
    g34, g2, g53, g5 = call(
        pick_kernel,
        (pos, offsets),
        (mkv, rkv),
        [rows(384), rows(512), rows(320), rows(64)],
        [pltpu.VMEM((4, CHIP, HD), F32)],
        unread=(state[0],),
    )
    zb = swap(g34, Z)
    a0, a1, a2 = swap(g53, X1), swap(g5, X2), swap(g5, X1 | X2)
    z2 = swap(g2, Z)
    state = call(
        other_tile_kernel, (pos,), (*state, rq, rkv), states, flops=2 * unit, unread=(g34,), inplace=3
    )
    p1, p2 = call(pair_kernel, (), (g34, zb), [rows(512), rows(256)])
    h1, h2, h3 = swap(p1, X1), swap(p2, X2), swap(p2, X1 | X2)
    x5 = call(gather_kernel, (), (g5, a0, a1, a2), [rows(256)], unread=(state[0],))[0]
    e, f, g = swap(x5, Z), swap(x5, Y1), swap(x5, Y1 | Z)
    *state, bq = call(
        near_kernel,
        (pos, offsets),
        (*state, mq, mkv, rq, rkv, g2, z2),
        states + [((448, HD), BF16)],
        [pltpu.VMEM((6, CHIP, HD), F32)],
        flops=3 * unit,
        unread=(x5,),
        inplace=3,
    )
    acc, _, total, other = call(
        far_kernel,
        (pos, offsets),
        (*state, bq, g34, g5, a0, a1, a2, zb, h1, h2, h3, e, f, g),
        states + [rows(TOK)],
        flops=unit,
        inplace=3,
    )
    back = swap(other, CORE)

    half = (256, TOK)
    mine, opposite = call(
        mine_kernel, (pos,), (acc, total, w), [rows(TOK), ((TOK, TOK), F32)], flops=TOK**3, unread=(other,)
    )
    up1, down1 = call(opposite_kernel, (pos,), (opposite, back, w), [(half, BF16)] * 2, flops=TOK**3)
    came_up, came_down = cross(up1, 1), cross(down1, 3)
    up2, down2, up_late, down_late, own = call(
        rest_kernel,
        (pos,),
        (mine, back, w),
        [(half, BF16)] * 2 + [(half, F32)] * 2 + [((TOK, TOK), F32)],
        flops=6 * TOK**3,
        unread=(up1,),
    )
    up2, down2 = cross(up2, 1), cross(down2, 3)
    up3 = cross(call(relay_kernel, (), (up_late, came_up), [(half, BF16)])[0], 3)
    down3 = cross(call(relay_kernel, (), (down_late, came_down), [(half, BF16)])[0], 1)
    return call(
        final_kernel,
        (),
        (own, up2, up3, down2, down3),
        [((TOK, TOK), BF16)],
        [pltpu.VMEM((TOK, TOK), BF16), pltpu.SemaphoreType.DMA((4,))],
        outside=ANY,
    )[0]


def solution(mesh):
    placed = (P("ctx", "head"), P("ctx", "head"), P("ctx", "head"), P(), P("head", None))
    return jax.shard_map(
        local, mesh=mesh, in_specs=placed, out_specs=P("ctx", "head"), check_vma=False
    )
```

```python
import math

import jax
import jax.numpy as jnp
from jax import lax
from jax.experimental import pallas as pl
from jax.experimental.pallas import tpu as pltpu
from jax.sharding import PartitionSpec as P

HD = 128
F32 = jnp.float32
BF16 = jnp.bfloat16
TOK = 512
CHIP = 2 * TOK
MIB = 1024 * 1024
GAIN = math.log2(math.e) / math.sqrt(HD)
CORE, Z, X1, X2, Y1 = 1, 2, 4, 8, 16


def swap(block, bits):
    return lax.ppermute(block, "ctx", [(i, i ^ bits) for i in range(64)])


def cross(block, bits):
    return lax.ppermute(block, "head", [(i, i ^ bits) for i in range(4)])


def used(off, level, first=0, count=None):
    r = 1 << level
    n = CHIP // r if count is None else count
    return pl.ds(off + first * r, n, stride=r)


def halves(pos):
    here = pl.multiple_of(pos[0] * TOK, TOK)
    there = pl.multiple_of(TOK - pos[0] * TOK, TOK)
    return pl.ds(here, TOK), pl.ds(there, TOK)


def run_copies(moves, sems):
    copies = [pltpu.make_async_copy(src, dst, sems.at[i]) for i, (src, dst) in enumerate(moves)]
    for copy in copies:
        copy.start()
    for copy in copies:
        copy.wait()


def theirs_kernel(k, v, okv, sems):
    core = lax.rem(lax.axis_index("ctx"), 2)
    theirs = pl.ds(pl.multiple_of(256 - core * 256, 256), 256)
    run_copies([(k.at[:, theirs], okv.at[0]), (v.at[:, theirs], okv.at[1])], sems)


def mine_columns_kernel(q, k, v, after, oq, mkv, mq, sems):
    del after
    core = lax.rem(lax.axis_index("ctx"), 2)
    theirs = pl.ds(pl.multiple_of(256 - core * 256, 256), 256)
    mine = pl.ds(pl.multiple_of(core * 256, 256), 256)
    moves = [(q.at[:, theirs], oq), (q.at[:, mine], mq)]
    moves += [(k.at[:, mine], mkv.at[0]), (v.at[:, mine], mkv.at[1])]
    run_copies(moves, sems)


def fill(buf, base, pos, mine, theirs):
    here, there = halves(pos)
    for j in range(2):
        cols = slice(j * HD, (j + 1) * HD)
        buf[base + j, here, :] = mine[:, cols].astype(F32)
        buf[base + j, there, :] = theirs[:, cols].astype(F32)


def pick_kernel(pos, offs, mkv, rkv, g34, g2, g5, buf):
    for i in range(2):
        fill(buf, 2 * i, pos, mkv.at[i], rkv.at[i])
    for level, dst, row in ((5, g5, 0), (3, g34, 0), (4, g34, 256), (2, g2, 0)):
        n = CHIP >> level
        for j in range(2):
            rows = used(offs[level, pos[1] + j], level)
            for i in range(2):
                at = slice(row + j * n, row + (j + 1) * n)
                dst[at, i * HD : (i + 1) * HD] = buf[2 * i + j, rows, :].astype(BF16)


def raw_scores(q, k):
    return lax.dot_general(q, k, (((1,), (1,)), ((), ())), preferred_element_type=F32)


def softmax_parts(scores, values):
    peaks = [jnp.max(s, axis=-1, keepdims=True) for s in scores]
    expos = [jnp.exp2((s - m) * GAIN).astype(BF16) for s, m in zip(scores, peaks)]
    parts = []
    for m, e, v in zip(peaks, expos, values):
        wide = jnp.concatenate([v, jnp.ones_like(v)], axis=1)
        mixed = jnp.dot(e, wide, preferred_element_type=F32)
        parts.append((jnp.broadcast_to(m, (m.shape[0], HD)), mixed[:, HD:], mixed[:, :HD]))
    return parts


def causal_scores(q, k):
    row = lax.broadcasted_iota(jnp.int32, (256, 256), 0)
    col = lax.broadcasted_iota(jnp.int32, (256, 256), 1)
    first = jnp.where(col <= row, raw_scores(q[:256], k[:256]), -jnp.inf)
    last = jnp.where(col <= row, raw_scores(q[256:], k[256:]), -jnp.inf)
    return [first, jnp.concatenate([raw_scores(q[256:], k[:256]), last], axis=1)]


def merge(state, j, rows, part):
    acc, peak, total = state
    m, t, o = part
    old = peak[j, rows, :]
    top = jnp.maximum(old, m)
    a = jnp.exp2((old - top) * GAIN)
    b = jnp.exp2((m - top) * GAIN)
    acc[j, rows, :] = acc[j, rows, :] * a + o * b
    total[j, rows, :] = total[j, rows, :] * a + t * b
    peak[j, rows, :] = top


def tile(start, q, kv, state):
    acc, peak, total = state
    for j in range(2):
        cols = slice(j * HD, (j + 1) * HD)
        values = kv[1, :, cols]
        parts = softmax_parts(causal_scores(q[:, cols], kv[0, :, cols]), [values[:256], values])
        for half, (m, t, o) in enumerate(parts):
            rows = pl.ds(pl.multiple_of(start + half * 256, 256), 256)
            acc[j, rows, :] = o
            total[j, rows, :] = t
            peak[j, rows, :] = m


def other_tile_kernel(pos, q, kv, after, *state):
    del after
    tile(TOK - pos[0] * TOK, q, kv, state)


def own_tile_kernel(pos, acc0, peak0, total0, q, kv, after, *state):
    del acc0, peak0, total0, after
    tile(pos[0] * TOK, q, kv, state)


def mix_kernel(g5, y5, g34, after, u0, u1):
    del after
    for dst in (u0, u1):
        dst[:64, :] = g5[...]
        dst[64:128, :] = y5[...]
    u0[128:, :] = g34[:256, :]


def gather_kernel(u1, a0, a1, a2, after, out):
    del after
    for i, part in enumerate((u1, a0, a1, a2)):
        out[128 * i : 128 * (i + 1), :] = part[:128, :]


def pair_kernel(g34, zb, after, p1, p2):
    del after
    for dst in (p1, p2):
        dst[:128, :] = g34[256:, :]
        dst[128:256, :] = zb[256:, :]
    p1[256:, :] = zb[:256, :]


def far_scores(pos, q, blocks, level):
    n = q.shape[0]
    span = lax.rem(pos[2], 1 << (level - 1))
    code = lax.broadcasted_iota(jnp.int32, (1, TOK), 1) // n
    if level == 5:
        code = (code & 6) | ((code & 1) << 3) | (code >> 3)
    bias = jnp.where((code == 0) | ((span ^ code) < span), 0.0, -jnp.inf)
    s = raw_scores(q, jnp.concatenate([x[:, :HD] for x in blocks], axis=0)) + bias
    row = lax.broadcasted_iota(jnp.int32, s.shape, 0)
    col = lax.broadcasted_iota(jnp.int32, s.shape, 1)
    return jnp.where((col < n) & (col > row), -jnp.inf, s)


def far_values(blocks):
    return jnp.concatenate([x[:, HD:] for x in blocks], axis=0)


def near_kernel(pos, offs, acc0, peak0, total0, mq, mkv, rq, rkv, g2, z2, after, acc, peak, total, bq, buf):
    del acc0, peak0, total0, after
    state = (acc, peak, total)
    fill(buf, 0, pos, mq, rq)
    for i in range(2):
        fill(buf, 2 + 2 * i, pos, mkv.at[i], rkv.at[i])
    row = 0
    for level in (5, 4, 3):
        n = CHIP >> level
        for j in range(2):
            bq[row : row + n, :] = buf[j, used(offs[level, pos[1] + j], level), :].astype(BF16)
            row += n
    for j in range(2):
        off = offs[1, pos[1] + j]
        qs, ks, vs = (buf[2 * i + j, used(off, 1), :].astype(BF16) for i in range(3))
        parts = softmax_parts(causal_scores(qs, ks), [vs[:256], vs])
        for half, part in enumerate(parts):
            merge(state, j, used(off, 1, half * 256, 256), part)
    rows = [used(offs[2, pos[1] + j], 2) for j in range(2)]
    blocks = [[x[j * 256 : (j + 1) * 256] for x in (g2, z2)] for j in range(2)]
    scores = [far_scores(pos, buf[j, rows[j], :].astype(BF16), blocks[j], 2) for j in range(2)]
    parts = softmax_parts(scores, [far_values(b) for b in blocks])
    for j in range(2):
        merge(state, j, rows[j], parts[j])


def far_parts(pos, offs, bq, qrow, level, j, blocks):
    n = CHIP >> level
    rows = used(offs[level, pos[1] + j], level)
    scores = far_scores(pos, bq[qrow + j * n : qrow + (j + 1) * n, :], blocks, level)
    return j, rows, scores, far_values(blocks)


def merge_all(work, state):
    parts = softmax_parts([x[2] for x in work], [x[3] for x in work])
    for (j, rows, _, _), part in zip(work, parts):
        merge(state, j, rows, part)


def third_kernel(pos, offs, acc0, peak0, total0, bq, g34, a0, zb, h1, *state):
    del acc0, peak0, total0
    work = []
    for j in range(2):
        at = slice(j * 128, (j + 1) * 128)
        blocks = [g34[at], zb[at], a0[128 + j * 128 : 256 + j * 128], h1[256 + j * 128 : 384 + j * 128]]
        work.append(far_parts(pos, offs, bq, 192, 3, j, blocks))
    merge_all(work, state)


def far_kernel(
    pos, offs, acc0, peak0, total0, bq, g34, u1, a0, a1, a2, zb, h1, h2, h3, e, acc, peak, total, other
):
    del acc0, peak0, total0
    work = []
    for level, qrow in ((4, 64), (5, 0)):
        n = CHIP >> level
        for j in range(2):

            def cut(ref, row):
                return ref[row + j * n : row + (j + 1) * n]

            if level == 4:
                blocks = [cut(g34, 256), cut(zb, 256)]
                blocks += [cut(x, row) for x in (h1, h2, h3) for row in (0, 128)]
            else:
                blocks = [cut(x, row) for x in (u1, a0, a1, a2) for row in (0, 64)]
                blocks += [cut(e, 64 * i) for i in range(8)]
            work.append(far_parts(pos, offs, bq, qrow, level, j, blocks))
    merge_all(work, (acc, peak, total))
    finish(acc, total, halves(pos)[1], other)


def finish(acc, total, rows, dst):
    for j in range(2):
        dst[:, j * HD : (j + 1) * HD] = (acc[j, rows, :] * (1.0 / total[j, rows, :])).astype(BF16)


def dots(pos, far, rows, w, dest):
    start = 256 - pos[0] * 256 if far else pos[0] * 256
    at = pl.ds(pl.multiple_of(start, 256), 256)
    cols = pl.ds(pl.multiple_of(dest * TOK, TOK), TOK)
    return jnp.dot(rows, w[at, cols], preferred_element_type=F32)


def project(pos, mine, back, w, first, dest):
    rows = slice(first, first + 256)
    return dots(pos, False, mine[rows, :], w, dest) + dots(pos, True, back[rows, :], w, dest)


def mine_kernel(pos, acc, total, w, after, mine, part):
    del after
    finish(acc, total, halves(pos)[0], mine)
    part[...] = dots(pos, False, mine[...], w, pos[3] ^ 2)


def opposite_kernel(pos, part, back, w, up, down):
    up[...] = (part[:256, :] + dots(pos, True, back[:256, :], w, pos[3] ^ 2)).astype(BF16)
    down[...] = (part[256:, :] + dots(pos, True, back[256:, :], w, pos[3] ^ 2)).astype(BF16)


def rest_kernel(pos, mine, back, w, after, up, down, up_late, down_late, own):
    del after
    up[...] = project(pos, mine, back, w, 0, pos[3] ^ 1).astype(BF16)
    down[...] = project(pos, mine, back, w, 256, pos[3] ^ 3).astype(BF16)
    up_late[...] = project(pos, mine, back, w, 0, pos[3] ^ 3)
    down_late[...] = project(pos, mine, back, w, 256, pos[3] ^ 1)
    for first in (0, 256):
        own[first : first + 256, :] = project(pos, mine, back, w, first, pos[3])


def relay_kernel(late, came, out):
    out[...] = (late[...] + came[...].astype(F32)).astype(BF16)


def final_kernel(own, up2, up3, down2, down3, out, buf, sems):
    copies = []
    for i in range(4):
        rows = slice(i * 128, (i + 1) * 128)
        part = slice(i % 2 * 128, i % 2 * 128 + 128)
        a, b = (up2, up3) if i < 2 else (down2, down3)
        buf[rows, :] = (own[rows, :] + a[part, :].astype(F32) + b[part, :].astype(F32)).astype(BF16)
        copy = pltpu.make_async_copy(buf.at[rows, :], out.at[rows, :], sems.at[i])
        copy.start()
        copies.append(copy)
    for copy in copies:
        copy.wait()


SMEM = pl.BlockSpec(memory_space=pltpu.SMEM)
VMEM = pl.BlockSpec(memory_space=pltpu.VMEM)
ANY = pl.BlockSpec(memory_space=pl.ANY)


def call(
    kernel, scalars, arrays, outs, scratch=(), flops=0, unread=(), inside=VMEM, outside=VMEM, inplace=0, grant=24
):
    nbytes = sum(a.size * a.dtype.itemsize for a in arrays)
    return pl.pallas_call(
        kernel,
        in_specs=[SMEM] * len(scalars) + [inside] * len(arrays) + [ANY] * len(unread),
        out_specs=[outside] * len(outs),
        out_shape=[jax.ShapeDtypeStruct(s, t) for s, t in outs],
        scratch_shapes=list(scratch),
        input_output_aliases={len(scalars) + i: i for i in range(inplace)},
        compiler_params=pltpu.CompilerParams(vmem_limit_bytes=grant * MIB),
        cost_estimate=pl.CostEstimate(flops=flops, bytes_accessed=nbytes, transcendentals=0),
    )(*scalars, *arrays, *unread)


def local(q, k, v, offsets, w):
    ctx = lax.axis_index("ctx")
    head = lax.axis_index("head")
    core = ctx % 2
    pos = jnp.stack([core, head * 4 + core * 2, ctx // 2, head]).astype(jnp.int32)
    unit = 4 * TOK * TOK * HD
    part = (TOK, 256)

    def rows(n):
        return ((n, 256), BF16)

    q, k, v = (pltpu.with_memory_space_constraint(x, pltpu.HBM) for x in (q, k, v))
    sems = pltpu.SemaphoreType.DMA
    okv = call(theirs_kernel, (), (k, v), [((2,) + part, BF16)], [sems((2,))], inside=ANY)[0]
    rkv = swap(okv, CORE)
    oq, mkv, mq = call(
        mine_columns_kernel,
        (),
        (q, k, v),
        [(part, BF16), ((2,) + part, BF16), (part, BF16)],
        [sems((4,))],
        inside=ANY,
        unread=(okv,),
    )
    rq = swap(oq, CORE)
    states = [((2, CHIP, HD), F32)] * 3
    g34, g2, g5 = call(
        pick_kernel,
        (pos, offsets),
        (mkv, rkv),
        [rows(384), rows(512), rows(64)],
        [pltpu.VMEM((4, CHIP, HD), F32)],
    )
    y5, zb, z2 = swap(g5, Y1), swap(g34, Z), swap(g2, Z)
    state = call(other_tile_kernel, (pos,), (rq, rkv), states, flops=2 * unit, unread=(g34,))
    u0, u1 = call(mix_kernel, (), (g5, y5, g34), [rows(384), rows(128)], unread=(state[0],))
    a0, a1, a2 = swap(u0, X1), swap(u1, X2), swap(u1, X1 | X2)
    p1, p2 = call(pair_kernel, (), (g34, zb), [rows(512), rows(256)], unread=(u1,))
    h1, h2, h3 = swap(p1, X1), swap(p2, X2), swap(p2, X1 | X2)
    state = call(
        own_tile_kernel, (pos,), (*state, mq, mkv), states, flops=2 * unit, unread=(p1,), inplace=3
    )
    x5 = call(gather_kernel, (), (u1, a0, a1, a2), [rows(512)], unread=(state[0],))[0]
    e = swap(x5, Z)
    *state, bq = call(
        near_kernel,
        (pos, offsets),
        (*state, mq, mkv, rq, rkv, g2, z2),
        states + [((448, HD), BF16)],
        [pltpu.VMEM((6, CHIP, HD), F32)],
        flops=3 * unit,
        unread=(x5,),
        inplace=3,
    )
    state = call(
        third_kernel, (pos, offsets), (*state, bq, g34, a0, zb, h1), states, flops=unit // 2, inplace=3
    )
    acc, _, total, other = call(
        far_kernel,
        (pos, offsets),
        (*state, bq, g34, u1, a0, a1, a2, zb, h1, h2, h3, e),
        states + [rows(TOK)],
        flops=unit,
        inplace=3,
    )
    back = swap(other, CORE)

    half = (256, TOK)
    mine, opposite = call(
        mine_kernel, (pos,), (acc, total, w), [rows(TOK), ((TOK, TOK), F32)], flops=TOK**3, unread=(other,)
    )
    up1, down1 = call(opposite_kernel, (pos,), (opposite, back, w), [(half, BF16)] * 2, flops=TOK**3)
    came_up, came_down = cross(up1, 1), cross(down1, 3)
    up2, down2, up_late, down_late, own = call(
        rest_kernel,
        (pos,),
        (mine, back, w),
        [(half, BF16)] * 2 + [(half, F32)] * 2 + [((TOK, TOK), F32)],
        flops=6 * TOK**3,
        unread=(up1,),
    )
    up2, down2 = cross(up2, 1), cross(down2, 3)
    up3 = cross(call(relay_kernel, (), (up_late, came_up), [(half, BF16)])[0], 3)
    down3 = cross(call(relay_kernel, (), (down_late, came_down), [(half, BF16)])[0], 1)
    return call(
        final_kernel,
        (),
        (own, up2, up3, down2, down3),
        [((TOK, TOK), BF16)],
        [pltpu.VMEM((TOK, TOK), BF16), pltpu.SemaphoreType.DMA((4,))],
        outside=ANY,
    )[0]


def solution(mesh):
    placed = (P("ctx", "head"), P("ctx", "head"), P("ctx", "head"), P(), P("head", None))
    return jax.shard_map(
        local, mesh=mesh, in_specs=placed, out_specs=P("ctx", "head"), check_vma=False
    )
```

```python
import math

import jax
import jax.numpy as jnp
from jax import lax
from jax.experimental import pallas as pl
from jax.experimental.pallas import tpu as pltpu
from jax.sharding import PartitionSpec as P

HD = 128
F32 = jnp.float32
BF16 = jnp.bfloat16
TOK = 512
CHIP = 2 * TOK
MIB = 1024 * 1024
GAIN = math.log2(math.e) / math.sqrt(HD)
CORE, Z, X1, X2, Y1 = 1, 2, 4, 8, 16


def swap(block, bits):
    return lax.ppermute(block, "ctx", [(i, i ^ bits) for i in range(64)])


def cross(block, bits):
    return lax.ppermute(block, "head", [(i, i ^ bits) for i in range(4)])


def used(off, level, first=0, count=None):
    r = 1 << level
    n = CHIP // r if count is None else count
    return pl.ds(off + first * r, n, stride=r)


def halves(pos):
    here = pl.multiple_of(pos[0] * TOK, TOK)
    there = pl.multiple_of(TOK - pos[0] * TOK, TOK)
    return pl.ds(here, TOK), pl.ds(there, TOK)


def run_copies(moves, sems):
    copies = [pltpu.make_async_copy(src, dst, sems.at[i]) for i, (src, dst) in enumerate(moves)]
    for copy in copies:
        copy.start()
    for copy in copies:
        copy.wait()


def theirs_kernel(k, v, okv, sems):
    core = lax.rem(lax.axis_index("ctx"), 2)
    theirs = pl.ds(pl.multiple_of(256 - core * 256, 256), 256)
    run_copies([(k.at[:, theirs], okv.at[0]), (v.at[:, theirs], okv.at[1])], sems)


def mine_columns_kernel(q, k, v, after, oq, mkv, mq, sems):
    del after
    core = lax.rem(lax.axis_index("ctx"), 2)
    theirs = pl.ds(pl.multiple_of(256 - core * 256, 256), 256)
    mine = pl.ds(pl.multiple_of(core * 256, 256), 256)
    moves = [(q.at[:, theirs], oq), (q.at[:, mine], mq)]
    moves += [(k.at[:, mine], mkv.at[0]), (v.at[:, mine], mkv.at[1])]
    run_copies(moves, sems)


def fill(buf, base, pos, mine, theirs):
    here, there = halves(pos)
    for j in range(2):
        cols = slice(j * HD, (j + 1) * HD)
        buf[base + j, here, :] = mine[:, cols].astype(F32)
        buf[base + j, there, :] = theirs[:, cols].astype(F32)


def pick_kernel(pos, offs, mkv, rkv, g34, g5, buf):
    for i in range(2):
        fill(buf, 2 * i, pos, mkv.at[i], rkv.at[i])
    pick(pos, offs, buf, ((5, g5, 0), (3, g34, 0), (4, g34, 256)))


def second_kernel(pos, offs, buf, g2):
    pick(pos, offs, buf, ((2, g2, 0),))


def pick(pos, offs, buf, places):
    for level, dst, row in places:
        n = CHIP >> level
        for j in range(2):
            rows = used(offs[level, pos[1] + j], level)
            for i in range(2):
                at = slice(row + j * n, row + (j + 1) * n)
                dst[at, i * HD : (i + 1) * HD] = buf[2 * i + j, rows, :].astype(BF16)


def raw_scores(q, k):
    return lax.dot_general(q, k, (((1,), (1,)), ((), ())), preferred_element_type=F32)


def softmax_parts(scores, values):
    peaks = [jnp.max(s, axis=-1, keepdims=True) for s in scores]
    expos = [jnp.exp2((s - m) * GAIN).astype(BF16) for s, m in zip(scores, peaks)]
    parts = []
    for m, e, v in zip(peaks, expos, values):
        wide = jnp.concatenate([v, jnp.ones_like(v)], axis=1)
        mixed = jnp.dot(e, wide, preferred_element_type=F32)
        parts.append((jnp.broadcast_to(m, (m.shape[0], HD)), mixed[:, HD:], mixed[:, :HD]))
    return parts


def causal_scores(q, k):
    row = lax.broadcasted_iota(jnp.int32, (256, 256), 0)
    col = lax.broadcasted_iota(jnp.int32, (256, 256), 1)
    first = jnp.where(col <= row, raw_scores(q[:256], k[:256]), -jnp.inf)
    last = jnp.where(col <= row, raw_scores(q[256:], k[256:]), -jnp.inf)
    return [first, jnp.concatenate([raw_scores(q[256:], k[:256]), last], axis=1)]


def merge(state, j, rows, part):
    acc, peak, total = state
    m, t, o = part
    old = peak[j, rows, :]
    top = jnp.maximum(old, m)
    a = jnp.exp2((old - top) * GAIN)
    b = jnp.exp2((m - top) * GAIN)
    acc[j, rows, :] = acc[j, rows, :] * a + o * b
    total[j, rows, :] = total[j, rows, :] * a + t * b
    peak[j, rows, :] = top


def tile(start, q, kv, state):
    acc, peak, total = state
    for j in range(2):
        cols = slice(j * HD, (j + 1) * HD)
        values = kv[1, :, cols]
        parts = softmax_parts(causal_scores(q[:, cols], kv[0, :, cols]), [values[:256], values])
        for half, (m, t, o) in enumerate(parts):
            rows = pl.ds(pl.multiple_of(start + half * 256, 256), 256)
            acc[j, rows, :] = o
            total[j, rows, :] = t
            peak[j, rows, :] = m


def other_tile_kernel(pos, q, kv, after, *state):
    del after
    tile(TOK - pos[0] * TOK, q, kv, state)


def own_tile_kernel(pos, acc0, peak0, total0, q, kv, after, *state):
    del acc0, peak0, total0, after
    tile(pos[0] * TOK, q, kv, state)


def mix_kernel(g5, y5, g34, after, u0, u1):
    del after
    for dst in (u0, u1):
        dst[:64, :] = g5[...]
        dst[64:128, :] = y5[...]
    u0[128:, :] = g34[:256, :]


def gather_kernel(u1, a0, a1, a2, after, out):
    del after
    for i, part in enumerate((u1, a0, a1, a2)):
        out[128 * i : 128 * (i + 1), :] = part[:128, :]


def pair_kernel(g34, zb, after, p1, p2):
    del after
    for dst in (p1, p2):
        dst[:128, :] = g34[256:, :]
        dst[128:256, :] = zb[256:, :]
    p1[256:, :] = zb[:256, :]


def far_scores(pos, q, blocks, level):
    n = q.shape[0]
    span = lax.rem(pos[2], 1 << (level - 1))
    code = lax.broadcasted_iota(jnp.int32, (1, TOK), 1) // n
    if level == 5:
        code = (code & 6) | ((code & 1) << 3) | (code >> 3)
    bias = jnp.where((code == 0) | ((span ^ code) < span), 0.0, -jnp.inf)
    s = raw_scores(q, jnp.concatenate([x[:, :HD] for x in blocks], axis=0)) + bias
    row = lax.broadcasted_iota(jnp.int32, s.shape, 0)
    col = lax.broadcasted_iota(jnp.int32, s.shape, 1)
    return jnp.where((col < n) & (col > row), -jnp.inf, s)


def far_values(blocks):
    return jnp.concatenate([x[:, HD:] for x in blocks], axis=0)


def near_kernel(pos, offs, acc0, peak0, total0, mq, rq, kv, g2, z2, after, acc, peak, total, bq, buf):
    del acc0, peak0, total0, after
    state = (acc, peak, total)
    fill(buf, 0, pos, mq, rq)
    row = 0
    for level in (5, 4, 3):
        n = CHIP >> level
        for j in range(2):
            bq[row : row + n, :] = buf[j, used(offs[level, pos[1] + j], level), :].astype(BF16)
            row += n
    for j in range(2):
        off = offs[1, pos[1] + j]
        refs = (buf.at[j], kv.at[j], kv.at[2 + j])
        qs, ks, vs = (x[used(off, 1), :].astype(BF16) for x in refs)
        parts = softmax_parts(causal_scores(qs, ks), [vs[:256], vs])
        for half, part in enumerate(parts):
            merge(state, j, used(off, 1, half * 256, 256), part)
    rows = [used(offs[2, pos[1] + j], 2) for j in range(2)]
    blocks = [[x[j * 256 : (j + 1) * 256] for x in (g2, z2)] for j in range(2)]
    scores = [far_scores(pos, buf[j, rows[j], :].astype(BF16), blocks[j], 2) for j in range(2)]
    parts = softmax_parts(scores, [far_values(b) for b in blocks])
    for j in range(2):
        merge(state, j, rows[j], parts[j])


def far_parts(pos, offs, bq, qrow, level, j, blocks):
    n = CHIP >> level
    rows = used(offs[level, pos[1] + j], level)
    scores = far_scores(pos, bq[qrow + j * n : qrow + (j + 1) * n, :], blocks, level)
    return j, rows, scores, far_values(blocks)


def merge_all(work, state):
    parts = softmax_parts([x[2] for x in work], [x[3] for x in work])
    for (j, rows, _, _), part in zip(work, parts):
        merge(state, j, rows, part)


def third_kernel(pos, offs, acc0, peak0, total0, bq, g34, a0, zb, h1, *state):
    del acc0, peak0, total0
    work = []
    for j in range(2):
        at = slice(j * 128, (j + 1) * 128)
        blocks = [g34[at], zb[at], a0[128 + j * 128 : 256 + j * 128], h1[256 + j * 128 : 384 + j * 128]]
        work.append(far_parts(pos, offs, bq, 192, 3, j, blocks))
    merge_all(work, state)


def far_kernel(
    pos, offs, acc0, peak0, total0, bq, g34, u1, a0, a1, a2, zb, h1, h2, h3, e, acc, peak, total, other
):
    del acc0, peak0, total0
    work = []
    for level, qrow in ((4, 64), (5, 0)):
        n = CHIP >> level
        for j in range(2):

            def cut(ref, row):
                return ref[row + j * n : row + (j + 1) * n]

            if level == 4:
                blocks = [cut(g34, 256), cut(zb, 256)]
                blocks += [cut(x, row) for x in (h1, h2, h3) for row in (0, 128)]
            else:
                blocks = [cut(x, row) for x in (u1, a0, a1, a2) for row in (0, 64)]
                blocks += [cut(e, 64 * i) for i in range(8)]
            work.append(far_parts(pos, offs, bq, qrow, level, j, blocks))
    merge_all(work, (acc, peak, total))
    finish(acc, total, halves(pos)[1], other)


def finish(acc, total, rows, dst):
    for j in range(2):
        dst[:, j * HD : (j + 1) * HD] = (acc[j, rows, :] * (1.0 / total[j, rows, :])).astype(BF16)


def dots(pos, far, rows, w, dest):
    start = 256 - pos[0] * 256 if far else pos[0] * 256
    at = pl.ds(pl.multiple_of(start, 256), 256)
    cols = pl.ds(pl.multiple_of(dest * TOK, TOK), TOK)
    return jnp.dot(rows, w[at, cols], preferred_element_type=F32)


def project(pos, mine, back, w, first, dest):
    rows = slice(first, first + 256)
    return dots(pos, False, mine[rows, :], w, dest) + dots(pos, True, back[rows, :], w, dest)


def mine_kernel(pos, acc, total, w, after, mine, part):
    del after
    finish(acc, total, halves(pos)[0], mine)
    part[...] = dots(pos, False, mine[...], w, pos[3] ^ 2)


def opposite_kernel(pos, part, back, w, up, down):
    up[...] = (part[:256, :] + dots(pos, True, back[:256, :], w, pos[3] ^ 2)).astype(BF16)
    down[...] = (part[256:, :] + dots(pos, True, back[256:, :], w, pos[3] ^ 2)).astype(BF16)


def rest_kernel(pos, mine, back, w, after, up, down, up_late, down_late, own):
    del after
    up[...] = project(pos, mine, back, w, 0, pos[3] ^ 1).astype(BF16)
    down[...] = project(pos, mine, back, w, 256, pos[3] ^ 3).astype(BF16)
    up_late[...] = project(pos, mine, back, w, 0, pos[3] ^ 3)
    down_late[...] = project(pos, mine, back, w, 256, pos[3] ^ 1)
    for first in (0, 256):
        own[first : first + 256, :] = project(pos, mine, back, w, first, pos[3])


def relay_kernel(late, came, out):
    out[...] = (late[...] + came[...].astype(F32)).astype(BF16)


def final_kernel(own, up2, up3, down2, down3, out, buf, sems):
    copies = []
    for i in range(4):
        rows = slice(i * 128, (i + 1) * 128)
        part = slice(i % 2 * 128, i % 2 * 128 + 128)
        a, b = (up2, up3) if i < 2 else (down2, down3)
        buf[rows, :] = (own[rows, :] + a[part, :].astype(F32) + b[part, :].astype(F32)).astype(BF16)
        copy = pltpu.make_async_copy(buf.at[rows, :], out.at[rows, :], sems.at[i])
        copy.start()
        copies.append(copy)
    for copy in copies:
        copy.wait()


SMEM = pl.BlockSpec(memory_space=pltpu.SMEM)
VMEM = pl.BlockSpec(memory_space=pltpu.VMEM)
ANY = pl.BlockSpec(memory_space=pl.ANY)


def call(
    kernel, scalars, arrays, outs, scratch=(), flops=0, unread=(), inside=VMEM, outside=VMEM, inplace=0, grant=24
):
    nbytes = sum(a.size * a.dtype.itemsize for a in arrays)
    return pl.pallas_call(
        kernel,
        in_specs=[SMEM] * len(scalars) + [inside] * len(arrays) + [ANY] * len(unread),
        out_specs=[outside] * len(outs),
        out_shape=[jax.ShapeDtypeStruct(s, t) for s, t in outs],
        scratch_shapes=list(scratch),
        input_output_aliases={len(scalars) + i: i for i in range(inplace)},
        compiler_params=pltpu.CompilerParams(vmem_limit_bytes=grant * MIB),
        cost_estimate=pl.CostEstimate(flops=flops, bytes_accessed=nbytes, transcendentals=0),
    )(*scalars, *arrays, *unread)


def local(q, k, v, offsets, w):
    ctx = lax.axis_index("ctx")
    head = lax.axis_index("head")
    core = ctx % 2
    pos = jnp.stack([core, head * 4 + core * 2, ctx // 2, head]).astype(jnp.int32)
    unit = 4 * TOK * TOK * HD
    part = (TOK, 256)

    def rows(n):
        return ((n, 256), BF16)

    q, k, v = (pltpu.with_memory_space_constraint(x, pltpu.HBM) for x in (q, k, v))
    sems = pltpu.SemaphoreType.DMA
    okv = call(theirs_kernel, (), (k, v), [((2,) + part, BF16)], [sems((2,))], inside=ANY)[0]
    rkv = swap(okv, CORE)
    oq, mkv, mq = call(
        mine_columns_kernel,
        (),
        (q, k, v),
        [(part, BF16), ((2,) + part, BF16), (part, BF16)],
        [sems((4,))],
        inside=ANY,
        unread=(okv,),
    )
    rq = swap(oq, CORE)
    states = [((2, CHIP, HD), F32)] * 3
    g34, g5, kv = call(
        pick_kernel,
        (pos, offsets),
        (mkv, rkv),
        [rows(384), rows(64), ((4, CHIP, HD), F32)],
    )
    g2 = call(second_kernel, (pos, offsets), (kv,), [rows(512)])[0]
    y5, zb, z2 = swap(g5, Y1), swap(g34, Z), swap(g2, Z)
    state = call(other_tile_kernel, (pos,), (rq, rkv), states, flops=2 * unit, unread=(g34,))
    u0, u1 = call(mix_kernel, (), (g5, y5, g34), [rows(384), rows(128)], unread=(state[0],))
    a0, a1, a2 = swap(u0, X1), swap(u1, X2), swap(u1, X1 | X2)
    p1, p2 = call(pair_kernel, (), (g34, zb), [rows(512), rows(256)], unread=(u1,))
    h1, h2, h3 = swap(p1, X1), swap(p2, X2), swap(p2, X1 | X2)
    state = call(
        own_tile_kernel, (pos,), (*state, mq, mkv), states, flops=2 * unit, unread=(p1,), inplace=3
    )
    x5 = call(gather_kernel, (), (u1, a0, a1, a2), [rows(512)], unread=(state[0],))[0]
    e = swap(x5, Z)
    *state, bq = call(
        near_kernel,
        (pos, offsets),
        (*state, mq, rq, kv, g2, z2),
        states + [((448, HD), BF16)],
        [pltpu.VMEM((2, CHIP, HD), F32)],
        flops=3 * unit,
        unread=(x5,),
        inplace=3,
    )
    state = call(
        third_kernel, (pos, offsets), (*state, bq, g34, a0, zb, h1), states, flops=unit // 2, inplace=3
    )
    acc, _, total, other = call(
        far_kernel,
        (pos, offsets),
        (*state, bq, g34, u1, a0, a1, a2, zb, h1, h2, h3, e),
        states + [rows(TOK)],
        flops=unit,
        inplace=3,
    )
    back = swap(other, CORE)

    half = (256, TOK)
    mine, opposite = call(
        mine_kernel, (pos,), (acc, total, w), [rows(TOK), ((TOK, TOK), F32)], flops=TOK**3, unread=(other,)
    )
    up1, down1 = call(opposite_kernel, (pos,), (opposite, back, w), [(half, BF16)] * 2, flops=TOK**3)
    came_up, came_down = cross(up1, 1), cross(down1, 3)
    up2, down2, up_late, down_late, own = call(
        rest_kernel,
        (pos,),
        (mine, back, w),
        [(half, BF16)] * 2 + [(half, F32)] * 2 + [((TOK, TOK), F32)],
        flops=6 * TOK**3,
        unread=(up1,),
    )
    up2, down2 = cross(up2, 1), cross(down2, 3)
    up3 = cross(call(relay_kernel, (), (up_late, came_up), [(half, BF16)])[0], 3)
    down3 = cross(call(relay_kernel, (), (down_late, came_down), [(half, BF16)])[0], 1)
    return call(
        final_kernel,
        (),
        (own, up2, up3, down2, down3),
        [((TOK, TOK), BF16)],
        [pltpu.VMEM((TOK, TOK), BF16), pltpu.SemaphoreType.DMA((4,))],
        outside=ANY,
    )[0]


def solution(mesh):
    placed = (P("ctx", "head"), P("ctx", "head"), P("ctx", "head"), P(), P("head", None))
    return jax.shard_map(
        local, mesh=mesh, in_specs=placed, out_specs=P("ctx", "head"), check_vma=False
    )
```

```python
import math

import jax
import jax.numpy as jnp
from jax import lax
from jax.experimental import pallas as pl
from jax.experimental.pallas import tpu as pltpu
from jax.sharding import PartitionSpec as P

HD = 128
F32 = jnp.float32
BF16 = jnp.bfloat16
TOK = 512
CHIP = 2 * TOK
MIB = 1024 * 1024
GAIN = math.log2(math.e) / math.sqrt(HD)
CORE, Z, X1, X2, Y1 = 1, 2, 4, 8, 16


def swap(block, bits):
    return lax.ppermute(block, "ctx", [(i, i ^ bits) for i in range(64)])


def cross(block, bits):
    return lax.ppermute(block, "head", [(i, i ^ bits) for i in range(4)])


def used(off, level, first=0, count=None):
    r = 1 << level
    n = CHIP // r if count is None else count
    return pl.ds(off + first * r, n, stride=r)


def halves(pos):
    here = pl.multiple_of(pos[0] * TOK, TOK)
    there = pl.multiple_of(TOK - pos[0] * TOK, TOK)
    return pl.ds(here, TOK), pl.ds(there, TOK)


def run_copies(moves, sems):
    copies = [pltpu.make_async_copy(src, dst, sems.at[i]) for i, (src, dst) in enumerate(moves)]
    for copy in copies:
        copy.start()
    for copy in copies:
        copy.wait()


def theirs_kernel(k, v, okv, sems):
    core = lax.rem(lax.axis_index("ctx"), 2)
    theirs = pl.ds(pl.multiple_of(256 - core * 256, 256), 256)
    run_copies([(k.at[:, theirs], okv.at[0]), (v.at[:, theirs], okv.at[1])], sems)


def mine_columns_kernel(q, k, v, after, oq, mkv, mq, sems):
    del after
    core = lax.rem(lax.axis_index("ctx"), 2)
    theirs = pl.ds(pl.multiple_of(256 - core * 256, 256), 256)
    mine = pl.ds(pl.multiple_of(core * 256, 256), 256)
    moves = [(q.at[:, theirs], oq), (q.at[:, mine], mq)]
    moves += [(k.at[:, mine], mkv.at[0]), (v.at[:, mine], mkv.at[1])]
    run_copies(moves, sems)


def fill(buf, base, pos, mine, theirs):
    here, there = halves(pos)
    for j in range(2):
        cols = slice(j * HD, (j + 1) * HD)
        buf[base + j, here, :] = mine[:, cols].astype(F32)
        buf[base + j, there, :] = theirs[:, cols].astype(F32)


def pick_kernel(pos, offs, mkv, rkv, g34, g5, buf):
    for i in range(2):
        fill(buf, 2 * i, pos, mkv.at[i], rkv.at[i])
    pick(pos, offs, buf, ((5, g5, 0), (3, g34, 0), (4, g34, 256)))


def second_kernel(pos, offs, buf, g2):
    pick(pos, offs, buf, ((2, g2, 0),))


def pick(pos, offs, buf, places):
    for level, dst, row in places:
        n = CHIP >> level
        for j in range(2):
            rows = used(offs[level, pos[1] + j], level)
            for i in range(2):
                at = slice(row + j * n, row + (j + 1) * n)
                dst[at, i * HD : (i + 1) * HD] = buf[2 * i + j, rows, :].astype(BF16)


def raw_scores(q, k):
    return lax.dot_general(q, k, (((1,), (1,)), ((), ())), preferred_element_type=F32)


def softmax_parts(scores, values):
    peaks = [jnp.max(s, axis=-1, keepdims=True) for s in scores]
    expos = [jnp.exp2((s - m) * GAIN).astype(BF16) for s, m in zip(scores, peaks)]
    parts = []
    for m, e, v in zip(peaks, expos, values):
        wide = jnp.concatenate([v, jnp.ones_like(v)], axis=1)
        mixed = jnp.dot(e, wide, preferred_element_type=F32)
        parts.append((jnp.broadcast_to(m, (m.shape[0], HD)), mixed[:, HD:], mixed[:, :HD]))
    return parts


def causal_scores(q, k):
    row = lax.broadcasted_iota(jnp.int32, (256, 256), 0)
    col = lax.broadcasted_iota(jnp.int32, (256, 256), 1)
    first = jnp.where(col <= row, raw_scores(q[:256], k[:256]), -jnp.inf)
    last = jnp.where(col <= row, raw_scores(q[256:], k[256:]), -jnp.inf)
    return [first, jnp.concatenate([raw_scores(q[256:], k[:256]), last], axis=1)]


def merge(state, j, rows, part):
    acc, peak, total = state
    m, t, o = part
    old = peak[j, rows, :]
    top = jnp.maximum(old, m)
    a = jnp.exp2((old - top) * GAIN)
    b = jnp.exp2((m - top) * GAIN)
    acc[j, rows, :] = acc[j, rows, :] * a + o * b
    total[j, rows, :] = total[j, rows, :] * a + t * b
    peak[j, rows, :] = top


def tile(start, q, kv, state):
    acc, peak, total = state
    for j in range(2):
        cols = slice(j * HD, (j + 1) * HD)
        values = kv[1, :, cols]
        parts = softmax_parts(causal_scores(q[:, cols], kv[0, :, cols]), [values[:256], values])
        for half, (m, t, o) in enumerate(parts):
            rows = pl.ds(pl.multiple_of(start + half * 256, 256), 256)
            acc[j, rows, :] = o
            total[j, rows, :] = t
            peak[j, rows, :] = m


def other_tile_kernel(pos, q, kv, after, *state):
    del after
    tile(TOK - pos[0] * TOK, q, kv, state)


def own_tile_kernel(pos, acc0, peak0, total0, q, kv, after, *state):
    del acc0, peak0, total0, after
    tile(pos[0] * TOK, q, kv, state)


def mix_kernel(g5, y5, g34, after, g2, u0, u1):
    del after, g2
    for dst in (u0, u1):
        dst[:64, :] = g5[...]
        dst[64:128, :] = y5[...]
    u0[128:, :] = g34[:256, :]


def gather_kernel(u1, a0, a1, a2, after, out):
    del after
    for i, part in enumerate((u1, a0, a1, a2)):
        out[128 * i : 128 * (i + 1), :] = part[:128, :]


def pair_kernel(g34, zb, after, p1, p2):
    del after
    for dst in (p1, p2):
        dst[:128, :] = g34[256:, :]
        dst[128:256, :] = zb[256:, :]
    p1[256:, :] = zb[:256, :]


def far_scores(pos, q, blocks, level):
    n = q.shape[0]
    span = lax.rem(pos[2], 1 << (level - 1))
    code = lax.broadcasted_iota(jnp.int32, (1, TOK), 1) // n
    if level == 5:
        code = (code & 6) | ((code & 1) << 3) | (code >> 3)
    bias = jnp.where((code == 0) | ((span ^ code) < span), 0.0, -jnp.inf)
    s = raw_scores(q, jnp.concatenate([x[:, :HD] for x in blocks], axis=0)) + bias
    row = lax.broadcasted_iota(jnp.int32, s.shape, 0)
    col = lax.broadcasted_iota(jnp.int32, s.shape, 1)
    return jnp.where((col < n) & (col > row), -jnp.inf, s)


def far_values(blocks):
    return jnp.concatenate([x[:, HD:] for x in blocks], axis=0)


def near_kernel(pos, offs, acc0, peak0, total0, mq, rq, kv, g2, z2, after, acc, peak, total, bq, buf):
    del acc0, peak0, total0, after
    state = (acc, peak, total)
    fill(buf, 0, pos, mq, rq)
    row = 0
    for level in (5, 4, 3):
        n = CHIP >> level
        for j in range(2):
            bq[row : row + n, :] = buf[j, used(offs[level, pos[1] + j], level), :].astype(BF16)
            row += n
    for j in range(2):
        off = offs[1, pos[1] + j]
        refs = (buf.at[j], kv.at[j], kv.at[2 + j])
        qs, ks, vs = (x[used(off, 1), :].astype(BF16) for x in refs)
        parts = softmax_parts(causal_scores(qs, ks), [vs[:256], vs])
        for half, part in enumerate(parts):
            merge(state, j, used(off, 1, half * 256, 256), part)
    rows = [used(offs[2, pos[1] + j], 2) for j in range(2)]
    blocks = [[x[j * 256 : (j + 1) * 256] for x in (g2, z2)] for j in range(2)]
    scores = [far_scores(pos, buf[j, rows[j], :].astype(BF16), blocks[j], 2) for j in range(2)]
    parts = softmax_parts(scores, [far_values(b) for b in blocks])
    for j in range(2):
        merge(state, j, rows[j], parts[j])


def far_parts(pos, offs, bq, qrow, level, j, blocks):
    n = CHIP >> level
    rows = used(offs[level, pos[1] + j], level)
    scores = far_scores(pos, bq[qrow + j * n : qrow + (j + 1) * n, :], blocks, level)
    return j, rows, scores, far_values(blocks)


def merge_all(work, state):
    parts = softmax_parts([x[2] for x in work], [x[3] for x in work])
    for (j, rows, _, _), part in zip(work, parts):
        merge(state, j, rows, part)


def third_kernel(pos, offs, acc0, peak0, total0, bq, g34, a0, zb, h1, *state):
    del acc0, peak0, total0
    work = []
    for j in range(2):
        at = slice(j * 128, (j + 1) * 128)
        blocks = [g34[at], zb[at], a0[128 + j * 128 : 256 + j * 128], h1[256 + j * 128 : 384 + j * 128]]
        work.append(far_parts(pos, offs, bq, 192, 3, j, blocks))
    merge_all(work, state)


def far_kernel(
    pos, offs, acc0, peak0, total0, bq, g34, u1, a0, a1, a2, zb, h1, h2, h3, e, acc, peak, total, other
):
    del acc0, peak0, total0
    work = []
    for level, qrow in ((4, 64), (5, 0)):
        n = CHIP >> level
        for j in range(2):

            def cut(ref, row):
                return ref[row + j * n : row + (j + 1) * n]

            if level == 4:
                blocks = [cut(g34, 256), cut(zb, 256)]
                blocks += [cut(x, row) for x in (h1, h2, h3) for row in (0, 128)]
            else:
                blocks = [cut(x, row) for x in (u1, a0, a1, a2) for row in (0, 64)]
                blocks += [cut(e, 64 * i) for i in range(8)]
            work.append(far_parts(pos, offs, bq, qrow, level, j, blocks))
    merge_all(work, (acc, peak, total))
    finish(acc, total, halves(pos)[1], other)


def finish(acc, total, rows, dst):
    for j in range(2):
        dst[:, j * HD : (j + 1) * HD] = (acc[j, rows, :] * (1.0 / total[j, rows, :])).astype(BF16)


def dots(pos, far, rows, w, dest):
    start = 256 - pos[0] * 256 if far else pos[0] * 256
    at = pl.ds(pl.multiple_of(start, 256), 256)
    cols = pl.ds(pl.multiple_of(dest * TOK, TOK), TOK)
    return jnp.dot(rows, w[at, cols], preferred_element_type=F32)


def project(pos, mine, back, w, first, dest):
    rows = slice(first, first + 256)
    return dots(pos, False, mine[rows, :], w, dest) + dots(pos, True, back[rows, :], w, dest)


def mine_kernel(pos, acc, total, w, after, mine, part):
    del after
    finish(acc, total, halves(pos)[0], mine)
    part[...] = dots(pos, False, mine[...], w, pos[3] ^ 2)


def opposite_kernel(pos, part, back, w, up, down):
    up[...] = (part[:256, :] + dots(pos, True, back[:256, :], w, pos[3] ^ 2)).astype(BF16)
    down[...] = (part[256:, :] + dots(pos, True, back[256:, :], w, pos[3] ^ 2)).astype(BF16)


def rest_kernel(pos, mine, back, w, after, up, down, up_late, down_late, own):
    del after
    up[...] = project(pos, mine, back, w, 0, pos[3] ^ 1).astype(BF16)
    down[...] = project(pos, mine, back, w, 256, pos[3] ^ 3).astype(BF16)
    up_late[...] = project(pos, mine, back, w, 0, pos[3] ^ 3)
    down_late[...] = project(pos, mine, back, w, 256, pos[3] ^ 1)
    for first in (0, 256):
        own[first : first + 256, :] = project(pos, mine, back, w, first, pos[3])


def relay_kernel(late, came, out):
    out[...] = (late[...] + came[...].astype(F32)).astype(BF16)


def final_kernel(own, up2, up3, down2, down3, out, buf, sems):
    copies = []
    for i in range(4):
        rows = slice(i * 128, (i + 1) * 128)
        part = slice(i % 2 * 128, i % 2 * 128 + 128)
        a, b = (up2, up3) if i < 2 else (down2, down3)
        buf[rows, :] = (own[rows, :] + a[part, :].astype(F32) + b[part, :].astype(F32)).astype(BF16)
        copy = pltpu.make_async_copy(buf.at[rows, :], out.at[rows, :], sems.at[i])
        copy.start()
        copies.append(copy)
    for copy in copies:
        copy.wait()


SMEM = pl.BlockSpec(memory_space=pltpu.SMEM)
VMEM = pl.BlockSpec(memory_space=pltpu.VMEM)
ANY = pl.BlockSpec(memory_space=pl.ANY)


def call(
    kernel, scalars, arrays, outs, scratch=(), flops=0, unread=(), inside=VMEM, outside=VMEM, inplace=0, grant=24
):
    nbytes = sum(a.size * a.dtype.itemsize for a in arrays)
    return pl.pallas_call(
        kernel,
        in_specs=[SMEM] * len(scalars) + [inside] * len(arrays) + [ANY] * len(unread),
        out_specs=[outside] * len(outs),
        out_shape=[jax.ShapeDtypeStruct(s, t) for s, t in outs],
        scratch_shapes=list(scratch),
        input_output_aliases={len(scalars) + i: i for i in range(inplace)},
        compiler_params=pltpu.CompilerParams(vmem_limit_bytes=grant * MIB),
        cost_estimate=pl.CostEstimate(flops=flops, bytes_accessed=nbytes, transcendentals=0),
    )(*scalars, *arrays, *unread)


def local(q, k, v, offsets, w):
    ctx = lax.axis_index("ctx")
    head = lax.axis_index("head")
    core = ctx % 2
    pos = jnp.stack([core, head * 4 + core * 2, ctx // 2, head]).astype(jnp.int32)
    unit = 4 * TOK * TOK * HD
    part = (TOK, 256)

    def rows(n):
        return ((n, 256), BF16)

    q, k, v = (pltpu.with_memory_space_constraint(x, pltpu.HBM) for x in (q, k, v))
    sems = pltpu.SemaphoreType.DMA
    okv = call(theirs_kernel, (), (k, v), [((2,) + part, BF16)], [sems((2,))], inside=ANY)[0]
    rkv = swap(okv, CORE)
    oq, mkv, mq = call(
        mine_columns_kernel,
        (),
        (q, k, v),
        [(part, BF16), ((2,) + part, BF16), (part, BF16)],
        [sems((4,))],
        inside=ANY,
        unread=(okv,),
    )
    rq = swap(oq, CORE)
    states = [((2, CHIP, HD), F32)] * 3
    g34, g5, kv = call(
        pick_kernel,
        (pos, offsets),
        (mkv, rkv),
        [rows(384), rows(64), ((4, CHIP, HD), F32)],
    )
    g2 = call(second_kernel, (pos, offsets), (kv,), [rows(512)])[0]
    y5, zb, z2 = swap(g5, Y1), swap(g34, Z), swap(g2, Z)
    state = call(other_tile_kernel, (pos,), (rq, rkv), states, flops=2 * unit, unread=(g34,))
    u0, u1 = call(mix_kernel, (), (g5, y5, g34), [rows(384), rows(128)], unread=(state[0], g2))
    a0, a1, a2 = swap(u0, X1), swap(u1, X2), swap(u1, X1 | X2)
    p1, p2 = call(pair_kernel, (), (g34, zb), [rows(512), rows(256)], unread=(u1,))
    h1, h2, h3 = swap(p1, X1), swap(p2, X2), swap(p2, X1 | X2)
    state = call(
        own_tile_kernel, (pos,), (*state, mq, mkv), states, flops=2 * unit, unread=(p1,), inplace=3
    )
    x5 = call(gather_kernel, (), (u1, a0, a1, a2), [rows(512)], unread=(state[0],))[0]
    e = swap(x5, Z)
    *state, bq = call(
        near_kernel,
        (pos, offsets),
        (*state, mq, rq, kv, g2, z2),
        states + [((448, HD), BF16)],
        [pltpu.VMEM((2, CHIP, HD), F32)],
        flops=3 * unit,
        unread=(x5,),
        inplace=3,
    )
    state = call(
        third_kernel, (pos, offsets), (*state, bq, g34, a0, zb, h1), states, flops=unit // 2, inplace=3
    )
    acc, _, total, other = call(
        far_kernel,
        (pos, offsets),
        (*state, bq, g34, u1, a0, a1, a2, zb, h1, h2, h3, e),
        states + [rows(TOK)],
        flops=unit,
        inplace=3,
    )
    back = swap(other, CORE)

    half = (256, TOK)
    mine, opposite = call(
        mine_kernel, (pos,), (acc, total, w), [rows(TOK), ((TOK, TOK), F32)], flops=TOK**3, unread=(other,)
    )
    up1, down1 = call(opposite_kernel, (pos,), (opposite, back, w), [(half, BF16)] * 2, flops=TOK**3)
    came_up, came_down = cross(up1, 1), cross(down1, 3)
    up2, down2, up_late, down_late, own = call(
        rest_kernel,
        (pos,),
        (mine, back, w),
        [(half, BF16)] * 2 + [(half, F32)] * 2 + [((TOK, TOK), F32)],
        flops=6 * TOK**3,
        unread=(up1,),
    )
    up2, down2 = cross(up2, 1), cross(down2, 3)
    up3 = cross(call(relay_kernel, (), (up_late, came_up), [(half, BF16)])[0], 3)
    down3 = cross(call(relay_kernel, (), (down_late, came_down), [(half, BF16)])[0], 1)
    return call(
        final_kernel,
        (),
        (own, up2, up3, down2, down3),
        [((TOK, TOK), BF16)],
        [pltpu.VMEM((TOK, TOK), BF16), pltpu.SemaphoreType.DMA((4,))],
        outside=ANY,
    )[0]


def solution(mesh):
    placed = (P("ctx", "head"), P("ctx", "head"), P("ctx", "head"), P(), P("head", None))
    return jax.shard_map(
        local, mesh=mesh, in_specs=placed, out_specs=P("ctx", "head"), check_vma=False
    )
```
